512 devices in a mesh: kb: 32 (over z, y_lo), vir: 16 (over x, y_hi, core).
Axes of the slice: x: 4, y: 8 (y_hi: 2, y_lo: 4; y = y_hi * 4 + y_lo), z: 8, core: 2. Of those that a mesh axis runs over, the one named last changes fastest.
Arguments:
- amps: bfloat16 [32, 120, 160, 160], P('kb', None, 'vir'), may hold values from -6 to 6
- ints_pair: bfloat16 [64, 160, 16, 160], P('kb', None, None, 'vir'), may hold values from -0.5 to 0.5
- ints_fold: bfloat16 [64, 16, 160, 160], P('kb'), may hold values from -0.125 to 0.125
- eps_occ: float32 [64, 16], replicated, may hold values from -2 to -0.3
- eps_vir: float32 [64, 160], replicated, may hold values from 0.3 to 3
- kconserve: int32 [64, 64], replicated, may hold values from 0 to 63, as said below
- plan: int32 [2], replicated, may hold values from 0 to 63
Outputs:
- residual: bfloat16 [32, 120, 160, 160], P('kb', None, 'vir')
The draws below stay inside these ranges and needn't reach their ends.
Inputs may be any that keep to these rules, and one draw needn't show every extreme that they name: kconserve[k1, k3] labels the mesh point of momentum k1 - k3 modulo the 4 x 4 x 4 mesh under a labelling of the points drawn from the seed; each row and each column is a permutation.
All inputs are finite; a program needn't handle non-finite values.
Results may differ from the reference program's by a relative error of at most 0.0049.
Values may be sent and summed in bfloat16 or wider, within the bound.
A program may use at most 64 MiB of HBM per device.

```python
import jax
import jax.numpy as jnp
import numpy as np

OCC = 16
V = 160
KMESH = 4
STEPS = 2
NK = 64
PAIRS = 120
KBLOCKS = 32
N_KB = 32


def draw_kconserve(key, part):
    labels = jax.random.permutation(jax.random.fold_in(key, 7), NK)
    inverse = jnp.argsort(labels).astype(jnp.int32)
    coord_x = labels // (KMESH * KMESH)
    coord_y = labels // KMESH % KMESH
    coord_z = labels % KMESH
    diff_x = (coord_x[:, None] - coord_x[None, :]) % KMESH
    diff_y = (coord_y[:, None] - coord_y[None, :]) % KMESH
    diff_z = (coord_z[:, None] - coord_z[None, :]) % KMESH
    point = (diff_x * KMESH + diff_y) * KMESH + diff_z
    return inverse[point].astype(jnp.int32)


def steps_of(rng, extent, split, low, high):
    factor_of, own = 1.0, jax.random.fold_in(rng, 6)
    for axis_at, blocks in split:
        heights = jnp.exp(jax.random.uniform(jax.random.fold_in(own, axis_at), (blocks,), jnp.float32, low / len(split), high / len(split)))
        factor_of = factor_of * jnp.repeat(heights, extent[axis_at] // blocks).reshape([-1 if axis == axis_at else 1 for axis in range(len(extent))])
    return factor_of


def bell_draw(key, extent, deviation, limit, split=(), held_as=jnp.bfloat16):
    loudness = steps_of(key, extent, split, -0.22, 0.18) if split else 1.0
    array = jax.random.normal(key, extent, jnp.float32) * deviation * loudness
    return jnp.minimum(jnp.maximum(array, -limit), limit).astype(held_as)


def setup_inputs(seed: int = 0) -> dict:
    key_list = jax.random.split(jax.random.key(seed), 8)
    return {
        "amps": bell_draw(key_list[0], (KBLOCKS, PAIRS, V, V), 1.0, 6.0, ((0, 32), (2, 16))),
        "ints_pair": bell_draw(key_list[1], (NK, V, OCC, V), V ** -0.5, 0.5, ((0, 32), (3, 16))),
        "ints_fold": bell_draw(key_list[2], (NK, OCC, V, V), (OCC * V) ** -0.5, 0.125, ((0, 32),)),
        "eps_occ": jnp.clip(jax.random.uniform(key_list[3], (NK, OCC), jnp.float32, -2.0, -0.3), -2.0, -0.3),
        "eps_vir": jnp.clip(jax.random.uniform(key_list[4], (NK, V), jnp.float32, 0.3, 3.0), 0.3, 3.0),
        "kconserve": draw_kconserve(jax.random.fold_in(key_list[7], 71), 0),
        "plan": jax.random.randint(key_list[6], (STEPS,), 0, NK).astype(jnp.int32),
    }


def reference(amps, ints_pair, ints_fold, eps_occ, eps_vir, kconserve, plan):
    kdev = NK // N_KB
    first_idx, second_idx = np.triu_indices(OCC, 1)
    blocks = []
    for block in range(N_KB):
        kfirst = block * kdev
        rows = amps[block].reshape(PAIRS * V, V)
        pair_eps = eps_occ[kfirst][first_idx] + eps_occ[kfirst][second_idx]
        left_den = (eps_vir[kfirst][None, :] - pair_eps[:, None]).reshape(PAIRS * V, 1)
        total = jnp.zeros((PAIRS * V, V), jnp.float32)
        for step in range(STEPS):
            kthird = plan[step]
            ksecond = kconserve[kfirst, kthird]
            zeta = jnp.dot(rows, ints_pair[kthird].reshape(V, OCC * V), preferred_element_type=jnp.float32)
            right_den = (eps_vir[ksecond][None, :] - eps_occ[kthird][:, None]).reshape(1, OCC * V)
            triples = (zeta / (left_den + right_den)).astype(jnp.bfloat16)
            total = total + jnp.dot(triples, ints_fold[kthird].reshape(OCC * V, V), preferred_element_type=jnp.float32)
        blocks.append(total.reshape(PAIRS, V, V).astype(jnp.bfloat16))
    return jnp.stack(blocks, 0)
```

```python
import functools

import jax
import jax.numpy as jnp
import numpy as np
from jax import lax
from jax.experimental import pallas as pl
from jax.experimental.pallas import tpu as pltpu
from jax.sharding import PartitionSpec as P

STEPS = 2
TILES = 25
MESH = pl.DeviceIdType.MESH
F32 = jnp.float32
BF16 = jnp.bfloat16
NT = (((1,), (1,)), ((), ()))
TN = (((0,), (0,)), ((), ()))


def iota(shape, dim):
    return lax.broadcasted_iota(jnp.int32, shape, dim)


def onehot(mask):
    return jnp.where(mask, 1.0, 0.0).astype(BF16)


def prep_kernel(plan, kcons, amps, pair, fold, occt, evir, x_out, l_out, left_out, right_out):
    kb = lax.axis_index("kb")
    vir = lax.axis_index("vir")
    kfirst = 2 * kb
    pick = onehot(
        (iota((160, 2560), 0) % 16 == iota((160, 2560), 1) // 160)
        & (iota((160, 2560), 1) % 160 == 10 * vir + iota((160, 2560), 0) // 16)
    )
    row, col = iota((160, 128), 0), iota((160, 128), 1)
    tail = [onehot((row - 128 == col - 32 * j) & (row >= 128)) for j in range(4)]
    dot = functools.partial(jnp.dot, preferred_element_type=F32)
    for s in range(STEPS):
        slot = plan[s] % 2
        p = pair[slot].reshape(5, 2, 16, 160)
        f = dot(pick, fold[slot].reshape(2560, 160)).astype(BF16).reshape(5, 2, 16, 160)
        parts = [p[:, 0], p[:, 1], f[:, 0], f[:, 1]]
        for j in range(4):
            x_out[5 * j:5 * j + 5, s] = parts[j][:, :, :128]
        flat = [q.reshape(80, 160) for q in (p[:, 0], f[:, 0], p[:, 1], f[:, 1])]
        rem = sum(dot(flat[j], tail[j]) for j in range(4))
        x_out[20:25, s] = rem.astype(BF16).reshape(5, 16, 128)
    l_out[...] = jnp.zeros_like(l_out)
    for q in range(2):
        place = onehot(
            iota((160, 256), 0) + jnp.where(iota((160, 256), 0) >= 128, 64 * q, 0) == iota((160, 256), 1)
        )
        for a in range(10):
            l_out[q, a, :120] = lax.dot_general(amps[a], place, TN, preferred_element_type=F32).astype(BF16)
    row = iota((128, 16), 0)
    band = iota((128, 16), 1)
    member = jnp.zeros((128, 16), jnp.bool_)
    start = 0
    for i in range(16):
        n = 15 - i
        inside = (row >= start) & (row < start + n)
        member = member | (inside & ((band == i) | (band == i + 1 + row - start)))
        start += n
    sums = jnp.dot(jnp.where(member, 1.0, 0.0), occt[...], precision=lax.Precision.HIGHEST, preferred_element_type=F32)
    pe = jnp.sum(jnp.where(iota((128, 64), 1) == kfirst, sums, 0.0), axis=1, keepdims=True)
    vrow = evir[pl.ds(kfirst, 1), :]
    for a in range(10):
        mine = jnp.sum(jnp.where(iota((1, 160), 1) == 10 * vir + a, vrow, 0.0), axis=1, keepdims=True)
        left_out[a] = jnp.broadcast_to(mine - pe, (128, 128))
    r = iota((24, 128), 0)
    lane = iota((24, 128), 1)
    rq, rp, rt = r // 10, (r // 5) % 2, r % 5
    v8 = lane // 16
    xx = jnp.where(rp == 0, v8 // 2, v8 % 4)
    yh = jnp.where(rp == 0, v8 % 2, v8 // 4)
    col = jnp.minimum(10 * ((xx * 2 + yh) * 2 + rp) + 2 * rt + rq, 159)
    occ16 = lax.dot_general(
        occt[...], jnp.where(iota((16, 128), 1) % 16 == iota((16, 128), 0), 1.0, 0.0), TN,
        precision=lax.Precision.HIGHEST, preferred_element_type=F32)
    for s in range(STEPS):
        k3 = plan[s]
        k2 = kcons[kfirst, k3]
        vs = evir[pl.ds(k2, 1), :]
        low = jnp.broadcast_to(vs[:, :128], (24, 128))
        high = jnp.broadcast_to(vs[:, 32:160], (24, 128))
        got = jnp.where(
            col < 128,
            jnp.take_along_axis(low, jnp.minimum(col, 127), axis=1),
            jnp.take_along_axis(high, jnp.maximum(col - 32, 0), axis=1),
        )
        occ = jnp.sum(jnp.where(iota((64, 128), 0) == k3, occ16, 0.0), axis=0, keepdims=True)
        right_out[s] = got - occ


def main_kernel(plan, x, l_ref, left, right, out,
                cand, buf, pq, fq, acc,
                s1, r1, s2, r2, s3, r3, s4, r4, s5, r5):
    kb = lax.axis_index("kb")
    vir = lax.axis_index("vir")
    z, yl = kb // 4, kb % 4
    xx, yh, core = vir // 4, (vir // 2) % 2, vir % 2
    y = yh * 4 + yl
    f = y + core * (z - y)
    l = z + core * (y - z)

    def dev(x_, f_, l_):
        y_ = f_ + core * (l_ - f_)
        z_ = l_ + core * (f_ - l_)
        return (z_ * 4 + y_ % 4, (x_ * 2 + y_ // 4) * 2 + core)

    sibling = (kb, vir + 1 - 2 * core)
    rnext = dev(xx, f, (l + 1) % 8)
    lnext = dev(xx, f, (l + 7) % 8)

    barrier = pltpu.get_barrier_semaphore()

    def greet(d):
        pl.semaphore_signal(barrier, inc=1, device_id=d, device_id_type=MESH)

    @pl.loop(1, 32)
    def _(i):
        greet(((kb + i) % 32, vir))

    @pl.loop(1, 8)
    def _(i):
        greet(dev(xx, (f + i) % 8, l))

    @pl.loop(1, 4)
    def _(i):
        greet(dev((xx + i) % 4, f, l))

    greet(rnext)
    greet(lnext)
    greet(sibling)
    pl.semaphore_wait(barrier, 31 + 7 + 3 + 2 + 1)

    def remote(src, dst, ss, rs, d):
        return pltpu.make_async_remote_copy(
            src_ref=src, dst_ref=dst, send_sem=ss, recv_sem=rs, device_id=d, device_id_type=MESH)

    def copy1(i, target, slot):
        return remote(x.at[target], cand.at[slot], s1.at[i], r1.at[i], (target, vir))

    @pl.loop(1, 32)
    def _(i):
        target = (kb + i) % 32

        @pl.when(target < TILES)
        def _():
            copy1(i, target, kb).start()

    @pl.when(kb < TILES)
    def _():
        cand[kb] = x[kb]

        @pl.loop(1, 32)
        def _(i):
            copy1(i, kb, (kb + 32 - i) % 32).wait_recv()

        for s in range(STEPS):
            buf[core, s, l, xx, f] = cand[plan[s] // 2, s]

    @pl.when(kb >= TILES)
    def _():
        for s in range(STEPS):
            buf[core, s, l, xx, f] = jnp.zeros((16, 128), BF16)

    def copy2(i, slot):
        here = buf.at[core, :, l, xx, slot]
        return remote(here, here, s2.at[i], r2.at[i], dev(xx, (f + i) % 8, l))

    @pl.loop(1, 8)
    def _(i):
        copy2(i, f).start()

    @pl.loop(1, 8)
    def _(i):
        copy2(i, (f + 8 - i) % 8).wait_recv()

    def copy3(s, i, slot):
        here = buf.at[core, s, l, slot]
        return remote(here, here, s3.at[s, i], r3.at[s, i], dev((xx + i) % 4, f, l))

    for s in range(STEPS):
        for i in range(1, 4):
            copy3(s, i, xx).start()

    def copy4(s, t, way, half, origin):
        here = buf.at[core, s, origin, pl.ds(2 * half, 2)]
        return remote(here, here, s4.at[s, t, way, half], r4.at[s, t, way, half], lnext if way else rnext)

    def copy5(s, plane, origin, half):
        here = buf.at[plane, s, origin, pl.ds(2 * half, 2)]
        return remote(here, here, s5.at[s, origin, half], r5.at[s, origin, half], sibling)

    def begin(s):
        for i in range(1, 4):
            copy3(s, i, (xx + 4 - i) % 4).wait_recv()
        for half in range(2):
            for way in range(2):
                copy4(s, 0, way, half, l).start()
        for half in range(2):
            copy5(s, core, l, half).start()

    def hop(s, t):
        for half in range(2):
            for way in range(2):
                if t == 4 and way != half:
                    continue
                origin = (l + t) % 8 if way else (l + 8 - t) % 8
                copy4(s, t - 1, way, half, origin).wait_recv()
                if t < 3 or (t == 3 and way == half):
                    copy4(s, t, way, half, origin).start()
                copy5(s, core, origin, half).start()

    def finish(s):
        for half in range(2):
            @pl.loop(0, 8)
            def _(o, half=half):
                copy5(s, 1 - core, o, half).wait_recv()

    def tiles(s, base):
        got = []
        for plane in range(2):
            for tp in range(5):
                g = base + tp
                zz, ll = g // 4, g % 4
                if plane == 0:
                    got += [buf[0, s, zz, a, b * 4 + ll] for a in range(4) for b in range(2)]
                else:
                    got += [buf[1, s, b * 4 + ll, a, zz] for b in range(2) for a in range(4)]
        return got

    def assemble(s, q):
        for i, tile in enumerate(tiles(s, 5 * q)):
            pq[16 * i:16 * i + 16, :128] = tile
        for i, tile in enumerate(tiles(s, 10 + 5 * q)):
            fq[16 * i:16 * i + 16, :128] = tile
        for i, tile in enumerate(tiles(s, 20)):
            pq[16 * i:16 * i + 16, 128:] = tile
            fq[16 * i:16 * i + 16, 128:] = tile

    def block(s, q, m):
        rows = l_ref[q, pl.ds(2 * m, 2)].reshape(256, 256)
        lf = left[pl.ds(2 * m, 2)].reshape(256, 128)
        parts = []
        for j in range(5):
            zeta = lax.dot_general(rows, pq[256 * j:256 * j + 256, :], NT, preferred_element_type=F32)
            for i in range(2):
                r = 10 * q + 2 * j + i
                den = lf + right[s, r:r + 1, :]
                parts.append((zeta[:, 128 * i:128 * i + 128] / den).astype(BF16))
        return jnp.dot(jnp.concatenate(parts, axis=1), fq[...], preferred_element_type=F32)

    begin(0)
    begin(1)
    for t in range(1, 5):
        hop(0, t)
    finish(0)
    for t in range(1, 5):
        hop(1, t)

    for q in range(2):
        assemble(0, q)

        @pl.loop(0, 5)
        def _(m, q=q):
            acc[q, m] = block(0, q, m)

    finish(1)
    assemble(1, 0)

    @pl.loop(0, 5)
    def _(m):
        acc[0, m] += block(1, 0, m)

    assemble(1, 1)
    row = iota((160, 256), 0)
    pick = onehot(row + jnp.where(row >= 128, 32, 0) == iota((160, 256), 1))

    @pl.loop(0, 5)
    def _(m):
        odd = acc[1, m] + block(1, 1, m)
        even = acc[0, m]
        total = jnp.concatenate(
            [even[:, :128] + odd[:, :128], even[:, 128:] + pltpu.roll(odd[:, 128:], 64, 1)], axis=1
        ).astype(BF16)
        done = lax.dot_general(pick, total, NT, preferred_element_type=F32).astype(BF16)
        out[2 * m] = done[:, :120]
        out[2 * m + 1] = done[:, 128:248]

    @pl.loop(1, 32)
    def _(i):
        target = (kb + i) % 32

        @pl.when(target < TILES)
        def _():
            copy1(i, target, kb).wait_send()

    @pl.loop(1, 8)
    def _(i):
        copy2(i, f).wait_send()

    for s in range(STEPS):
        for i in range(1, 4):
            copy3(s, i, xx).wait_send()
        for t in range(4):
            for half in range(2):
                for way in range(2):
                    if t == 3 and way != half:
                        continue
                    origin = (l + t) % 8 if way else (l + 8 - t) % 8
                    copy4(s, t, way, half, origin).wait_send()
        for half in range(2):
            @pl.loop(0, 8)
            def _(o, half=half, s=s):
                copy5(s, core, o, half).wait_send()


def local(amps, ints_pair, ints_fold, eps_occ, eps_vir, kconserve, plan):
    at = jnp.transpose(amps, (0, 2, 3, 1))[0]
    pair = jnp.transpose(ints_pair, (0, 3, 2, 1))
    vmem = pl.BlockSpec(memory_space=pltpu.VMEM)
    smem = pl.BlockSpec(memory_space=pltpu.SMEM)
    x, rows, left, right = pl.pallas_call(
        prep_kernel,
        out_shape=(
            jax.ShapeDtypeStruct((TILES, 2, 16, 128), BF16),
            jax.ShapeDtypeStruct((2, 10, 128, 256), BF16),
            jax.ShapeDtypeStruct((10, 128, 128), F32),
            jax.ShapeDtypeStruct((2, 24, 128), F32),
        ),
        in_specs=[smem, smem] + [vmem] * 5,
        out_specs=(vmem,) * 4,
        compiler_params=pltpu.CompilerParams(vmem_limit_bytes=32 * 2**20),
        name="prep",
    )(plan, kconserve, at, pair, ints_fold, eps_occ.T, eps_vir)
    dma = pltpu.SemaphoreType.DMA
    out = pl.pallas_call(
        main_kernel,
        out_shape=jax.ShapeDtypeStruct((10, 160, 120), BF16),
        in_specs=[smem] + [vmem] * 4,
        out_specs=vmem,
        scratch_shapes=[
            pltpu.VMEM((32, 2, 16, 128), BF16),
            pltpu.VMEM((2, 2, 8, 4, 8, 16, 128), BF16),
            pltpu.VMEM((1280, 256), BF16),
            pltpu.VMEM((1280, 256), BF16),
            pltpu.VMEM((2, 5, 256, 256), F32),
            dma((32,)), dma((32,)),
            dma((8,)), dma((8,)),
            dma((2, 4)), dma((2, 4)),
            dma((2, 4, 2, 2)), dma((2, 4, 2, 2)),
            dma((2, 8, 2)), dma((2, 8, 2)),
        ],
        compiler_params=pltpu.CompilerParams(
            vmem_limit_bytes=40 * 2**20, collective_id=0, has_side_effects=True),
        name="triples",
    )(plan, x, rows, left, right)
    return jnp.transpose(out, (2, 0, 1))[None]


def solution(mesh):
    return jax.shard_map(
        local,
        mesh=mesh,
        in_specs=(
            P("kb", None, "vir", None),
            P("kb", None, None, "vir"),
            P("kb", None, None, None),
            P(),
            P(),
            P(),
            P(),
        ),
        out_specs=P("kb", None, "vir", None),
        check_vma=False,
    )
```

```python
import functools

import jax
import jax.numpy as jnp
import numpy as np
from jax import lax
from jax.experimental import pallas as pl
from jax.experimental.pallas import tpu as pltpu
from jax.sharding import PartitionSpec as P

STEPS = 2
TILES = 25
MESH = pl.DeviceIdType.MESH
F32 = jnp.float32
BF16 = jnp.bfloat16
NT = (((1,), (1,)), ((), ()))
TN = (((0,), (0,)), ((), ()))


def iota(shape, dim):
    return lax.broadcasted_iota(jnp.int32, shape, dim)


def onehot(mask):
    return jnp.where(mask, 1.0, 0.0).astype(BF16)


def kernel(plan, kcons, amps_any, pair_any, fold_any, occt_any, evir_any, out,
           amps, pair, fold, occt, evir, x, rows, left, right, cand, buf, pq, fq, acc,
           s0, s1, r1, s2, r2, s4, r4, s5, r5):
    kb = lax.axis_index("kb")
    vir = lax.axis_index("vir")
    z, yl = kb // 4, kb % 4
    xx, yh, core = vir // 4, (vir // 2) % 2, vir % 2
    y = yh * 4 + yl
    f = y + core * (z - y)
    l = z + core * (y - z)
    kfirst = 2 * kb

    def dev(x_, f_, l_):
        y_ = f_ + core * (l_ - f_)
        z_ = l_ + core * (f_ - l_)
        return (z_ * 4 + y_ % 4, (x_ * 2 + y_ // 4) * 2 + core)

    sibling = (kb, vir + 1 - 2 * core)
    rnext = dev(xx, f, (l + 1) % 8)
    lnext = dev(xx, f, (l + 7) % 8)

    low = pl.multiple_of(jnp.minimum(10 * vir // 16 * 16, 128), 16)
    loads = [
        pltpu.make_async_copy(fold_any.at[:, :, pl.ds(low, 32)], fold, s0.at[0]),
        pltpu.make_async_copy(pair_any, pair, s0.at[1]),
        pltpu.make_async_copy(amps_any, amps, s0.at[2]),
        pltpu.make_async_copy(occt_any, occt, s0.at[3]),
        pltpu.make_async_copy(evir_any, evir, s0.at[4]),
    ]
    for c in loads:
        c.start()

    barrier = pltpu.get_barrier_semaphore()

    def greet(d):
        pl.semaphore_signal(barrier, inc=1, device_id=d, device_id_type=MESH)

    def peer(i):
        return (xx + i // 8) % 4, (f + i) % 8

    @pl.loop(1, 32)
    def _(i):
        greet(((kb + i) % 32, vir))

    @pl.loop(1, 32)
    def _(i):
        a, b = peer(i)
        greet(dev(a, b, l))

    greet(rnext)
    greet(lnext)
    greet(sibling)

    pick = onehot(
        (iota((160, 512), 0) % 16 == iota((160, 512), 1) // 32)
        & (iota((160, 512), 1) % 32 + low == 10 * vir + iota((160, 512), 0) // 16)
    )
    row, col = iota((160, 128), 0), iota((160, 128), 1)
    tail = [onehot((row - 128 == col - 32 * j) & (row >= 128)) for j in range(4)]
    dot = functools.partial(jnp.dot, preferred_element_type=F32)
    loads[0].wait()
    loads[1].wait()
    for s in range(STEPS):
        slot = plan[s] % 2
        p = pair[slot].reshape(5, 2, 16, 160)
        g = dot(pick, fold[slot].reshape(512, 160)).astype(BF16).reshape(5, 2, 16, 160)
        parts = [p[:, 0], p[:, 1], g[:, 0], g[:, 1]]
        for j in range(4):
            x[5 * j:5 * j + 5, s] = parts[j][:, :, :128]
        rem = sum(dot(parts[i].reshape(80, 160), tail[j]) for j, i in enumerate((0, 2, 1, 3)))
        x[20:25, s] = rem.astype(BF16).reshape(5, 16, 128)

    pl.semaphore_wait(barrier, 31 + 31 + 2 + 1)

    def remote(src, dst, ss, rs, d):
        return pltpu.make_async_remote_copy(
            src_ref=src, dst_ref=dst, send_sem=ss, recv_sem=rs, device_id=d, device_id_type=MESH)

    def copy1(i, target, slot):
        return remote(x.at[target], cand.at[slot], s1.at[i], r1.at[i], (target, vir))

    @pl.loop(1, 32)
    def _(i):
        target = (kb + i) % 32

        @pl.when(target < TILES)
        def _():
            copy1(i, target, kb).start()

    loads[2].wait()
    rows[...] = jnp.zeros_like(rows)
    for q in range(2):
        e, to = iota((160, 256), 0), iota((160, 256), 1)
        place = onehot(e + jnp.where(e >= 128, 64 * q, 0) == to)
        for a in range(10):
            rows[q, a, :120] = lax.dot_general(amps[a], place, TN, preferred_element_type=F32).astype(BF16)
    loads[3].wait()
    loads[4].wait()
    row, band = iota((128, 16), 0), iota((128, 16), 1)
    member = jnp.zeros((128, 16), jnp.bool_)
    start = 0
    for i in range(16):
        inside = (row >= start) & (row < start + 15 - i)
        member = member | (inside & ((band == i) | (band == i + 1 + row - start)))
        start += 15 - i
    exact = dict(precision=lax.Precision.HIGHEST, preferred_element_type=F32)
    sums = jnp.dot(jnp.where(member, 1.0, 0.0), occt[...], **exact)
    pe = jnp.sum(jnp.where(iota((128, 64), 1) == kfirst, sums, 0.0), axis=1, keepdims=True)
    level = iota((64, 160), 0)
    vrow = jnp.sum(jnp.where(level == kfirst, evir[...], 0.0), axis=0, keepdims=True)
    for a in range(10):
        mine = jnp.sum(jnp.where(iota((1, 160), 1) == 10 * vir + a, vrow, 0.0), axis=1, keepdims=True)
        left[a] = jnp.broadcast_to(mine - pe, (128, 128))
    lane = iota((160, 256), 1)
    v8 = lane // 16 % 8
    v16 = jnp.where(lane < 128, 2 * v8, (v8 % 4 * 2 + v8 // 4) * 2 + 1)
    spread = jnp.where(iota((160, 256), 0) // 10 == v16, 1.0, 0.0)
    occ16 = lax.dot_general(
        occt[...], jnp.where(iota((16, 256), 1) % 16 == iota((16, 256), 0), 1.0, 0.0), TN, **exact)
    for s in range(STEPS):
        k3 = plan[s]
        k2 = kcons[kfirst, k3]
        vs = jnp.sum(jnp.where(level == k2, evir[...], 0.0), axis=0, keepdims=True)
        own = jnp.where(iota((16, 160), 1) % 10 == iota((16, 160), 0), vs, 0.0)
        occ = jnp.sum(jnp.where(iota((64, 256), 0) == k3, occ16, 0.0), axis=0, keepdims=True)
        right[s] = jnp.dot(own, spread, **exact) - occ

    @pl.when(kb < TILES)
    def _():
        cand[kb] = x[kb]

        @pl.loop(1, 32)
        def _(i):
            copy1(i, kb, (kb + 32 - i) % 32).wait_recv()

        for s in range(STEPS):
            buf[core, l, xx, f, s] = cand[plan[s] // 2, s]

    @pl.when(kb >= TILES)
    def _():
        for s in range(STEPS):
            buf[core, l, xx, f, s] = jnp.zeros((16, 128), BF16)

    def copy2(i, a, b):
        here = buf.at[core, l, a, b]
        to = peer(i)
        return remote(here, here, s2.at[i], r2.at[i], dev(*to, l))

    @pl.loop(1, 32)
    def _(i):
        copy2(i, xx, f).start()

    @pl.loop(1, 32)
    def _(i):
        copy2(i, (xx + 4 - i // 8) % 4, (f + 32 - i) % 8).wait_recv()

    def copy4(t, way, part, origin):
        here = buf.at[core, origin, part]
        return remote(here, here, s4.at[t, way, part], r4.at[t, way, part], lnext if way else rnext)

    def copy5(plane, origin, part):
        here = buf.at[plane, origin, part]
        return remote(here, here, s5.at[origin, part], r5.at[origin, part], sibling)

    for part in range(4):
        for way in range(2):
            copy4(0, way, part, l).start()
    for part in range(4):
        copy5(core, l, part).start()
    for t in range(1, 5):
        for part in range(4):
            for way in range(2):
                if t == 4 and way != part // 2:
                    continue
                origin = (l + t) % 8 if way else (l + 8 - t) % 8
                copy4(t - 1, way, part, origin).wait_recv()
                if t < 3 or (t == 3 and way == part // 2):
                    copy4(t, way, part, origin).start()
                copy5(core, origin, part).start()

    for part in range(4):
        @pl.loop(0, 8)
        def _(o, part=part):
            copy5(1 - core, o, part).wait_recv()

    def tiles(s, base):
        got = []
        for plane in range(2):
            for tp in range(5):
                g = base + tp
                zz, ll = g // 4, g % 4
                if plane == 0:
                    got += [buf[0, zz, a, b * 4 + ll, s] for a in range(4) for b in range(2)]
                else:
                    got += [buf[1, b * 4 + ll, a, zz, s] for b in range(2) for a in range(4)]
        return got

    def assemble(s, q):
        for i, tile in enumerate(tiles(s, 5 * q)):
            pq[16 * i:16 * i + 16, :128] = tile
        for i, tile in enumerate(tiles(s, 10 + 5 * q)):
            fq[16 * i:16 * i + 16, :128] = tile
        for i, tile in enumerate(tiles(s, 20)):
            pq[16 * i:16 * i + 16, 128:] = tile
            fq[16 * i:16 * i + 16, 128:] = tile

    def block(s, q, m):
        mine = rows[q, 5 * m:5 * m + 5].reshape(640, 256)
        lf = left[5 * m:5 * m + 5].reshape(640, 128)
        parts = []
        for j in range(5):
            zeta = lax.dot_general(mine, pq[256 * j:256 * j + 256, :], NT, preferred_element_type=F32)
            for i in range(2):
                plane, tp = (2 * j + i) // 5, (2 * j + i) % 5
                t = 2 * tp + q
                den = lf + right[s, t:t + 1, 128 * plane:128 * plane + 128]
                parts.append((zeta[:, 128 * i:128 * i + 128] / den).astype(BF16))
        return jnp.dot(jnp.concatenate(parts, axis=1), fq[...], preferred_element_type=F32)

    for q in range(2):
        assemble(0, q)
        for m in range(2):
            acc[q, m] = block(0, q, m)
    assemble(1, 0)
    for m in range(2):
        acc[0, m] += block(1, 0, m)
    assemble(1, 1)
    row = iota((160, 256), 0)
    back = onehot(row + jnp.where(row >= 128, 32, 0) == iota((160, 256), 1))
    for m in range(2):
        odd = acc[1, m] + block(1, 1, m)
        even = acc[0, m]
        total = jnp.concatenate(
            [even[:, :128] + odd[:, :128], even[:, 128:] + pltpu.roll(odd[:, 128:], 64, 1)], axis=1
        ).astype(BF16)
        done = lax.dot_general(back, total, NT, preferred_element_type=F32).astype(BF16)
        for a in range(5):
            out[5 * m + a] = done[:, 128 * a:128 * a + 120]

    @pl.loop(1, 32)
    def _(i):
        target = (kb + i) % 32

        @pl.when(target < TILES)
        def _():
            copy1(i, target, kb).wait_send()

    @pl.loop(1, 32)
    def _(i):
        copy2(i, xx, f).wait_send()

    for t in range(4):
        for part in range(4):
            for way in range(2):
                if t == 3 and way != part // 2:
                    continue
                origin = (l + t) % 8 if way else (l + 8 - t) % 8
                copy4(t, way, part, origin).wait_send()
    for part in range(4):
        @pl.loop(0, 8)
        def _(o, part=part):
            copy5(core, o, part).wait_send()


def local(amps, ints_pair, ints_fold, eps_occ, eps_vir, kconserve, plan):
    smem = pl.BlockSpec(memory_space=pltpu.SMEM)
    anywhere = pl.BlockSpec(memory_space=pl.ANY)
    dma = pltpu.SemaphoreType.DMA
    out = pl.pallas_call(
        kernel,
        out_shape=jax.ShapeDtypeStruct((10, 160, 120), BF16),
        in_specs=[smem, smem] + [anywhere] * 5,
        out_specs=pl.BlockSpec(memory_space=pltpu.VMEM),
        scratch_shapes=[
            pltpu.VMEM((10, 160, 120), BF16),
            pltpu.VMEM((2, 10, 16, 160), BF16),
            pltpu.VMEM((2, 16, 32, 160), BF16),
            pltpu.VMEM((16, 64), F32),
            pltpu.VMEM((64, 160), F32),
            pltpu.VMEM((TILES, 2, 16, 128), BF16),
            pltpu.VMEM((2, 10, 128, 256), BF16),
            pltpu.VMEM((10, 128, 128), F32),
            pltpu.VMEM((2, 16, 256), F32),
            pltpu.VMEM((32, 2, 16, 128), BF16),
            pltpu.VMEM((2, 8, 4, 8, 2, 16, 128), BF16),
            pltpu.VMEM((1280, 256), BF16),
            pltpu.VMEM((1280, 256), BF16),
            pltpu.VMEM((2, 2, 640, 256), F32),
            dma((5,)),
            dma((32,)), dma((32,)),
            dma((32,)), dma((32,)),
            dma((4, 2, 4)), dma((4, 2, 4)),
            dma((8, 4)), dma((8, 4)),
        ],
        compiler_params=pltpu.CompilerParams(
            vmem_limit_bytes=56 * 2**20, collective_id=0, has_side_effects=True),
        name="triples",
    )(plan, kconserve, jnp.transpose(amps, (0, 2, 3, 1))[0], jnp.transpose(ints_pair, (0, 3, 2, 1)),
      ints_fold, eps_occ.T, eps_vir)
    return jnp.transpose(out, (2, 0, 1))[None]


def solution(mesh):
    return jax.shard_map(
        local,
        mesh=mesh,
        in_specs=(
            P("kb", None, "vir", None),
            P("kb", None, None, "vir"),
            P("kb", None, None, None),
            P(),
            P(),
            P(),
            P(),
        ),
        out_specs=P("kb", None, "vir", None),
        check_vma=False,
    )
```

```python
import functools

import jax
import jax.numpy as jnp
import numpy as np
from jax import lax
from jax.experimental import pallas as pl
from jax.experimental.pallas import tpu as pltpu
from jax.sharding import PartitionSpec as P

STEPS = 2
UNITS = 10
MESH = pl.DeviceIdType.MESH
F32 = jnp.float32
BF16 = jnp.bfloat16
NT = (((1,), (1,)), ((), ()))
TN = (((0,), (0,)), ((), ()))


def iota(shape, dim):
    return lax.broadcasted_iota(jnp.int32, shape, dim)


def onehot(mask):
    return jnp.where(mask, 1.0, 0.0).astype(BF16)


def kernel(plan, kcons, amps_any, pair_any, fold_any, occt_any, evir_any, out,
           amps, pair, fold, occt, evir, x, rows, left, right, cand, buf, pq, fq, acc, part_out, part_in,
           s0, s1, r1, s2, r2, s3, r3, s4, r4, s5, r5):
    kb = lax.axis_index("kb")
    vir = lax.axis_index("vir")
    z, yl = kb >> 2, kb & 3
    xx, yh, core = vir >> 2, (vir >> 1) & 1, vir & 1
    y = yh * 4 + yl
    flip = core == 1
    f = jnp.where(flip, z, y)
    l = jnp.where(flip, y, z)
    kfirst = 2 * kb

    def dev(x_, f_, l_):
        y_ = jnp.where(flip, l_, f_)
        z_ = jnp.where(flip, f_, l_)
        return (z_ * 4 + (y_ & 3), x_ * 4 + (y_ >> 2) * 2 + core)

    def holder(t):
        v8 = xx * 2 + yh
        last = t >= 8
        z0 = jnp.where(last, v8, t)
        y0 = (z0 + v8 + jnp.where(last, t - 7, 0)) & 3
        z1 = jnp.where(last, (2 * xx + t - 4) & 7, t)
        y1 = jnp.where(last, xx, t >> 1)
        return jnp.where(flip, z1 * 4 + y1, z0 * 4 + y0)

    def source(u):
        last = u >= 8
        v8 = jnp.where(last, l, u)
        y0 = (v8 & 1) * 4 + ((l + v8 + jnp.where(last, u - 7, 0)) & 3)
        ll = l & 3
        x1 = jnp.where(last, ll, u & 3)
        z1 = jnp.where(last, (2 * ll + u - 4) & 7, 2 * ll + (u >> 2))
        return jnp.where(flip, x1, v8 >> 1), jnp.where(flip, z1, y0)

    v8 = xx * 2 + yh
    gap = (yl - z - v8) & 3
    extra0 = (z == v8) & ((gap == 1) | (gap == 2))
    main0 = gap == 0
    gap1 = (z - 2 * xx - 4) & 7
    extra1 = (xx == yl) & (gap1 < 2)
    main1 = (z >> 1) == yl
    main = jnp.where(flip, main1.astype(jnp.int32), main0.astype(jnp.int32))
    extra = jnp.where(flip, extra1.astype(jnp.int32), extra0.astype(jnp.int32))
    holds = main + extra
    slot_extra = jnp.where(flip, 8 + gap1, 7 + gap)
    slot_main = jnp.where(flip, (z & 1) * 4 + xx, v8)
    slot = jnp.where(main == 1, slot_main, jnp.where(extra == 1, slot_extra, 0))
    column = jnp.where(main == 1, z, jnp.where(extra == 1, slot_extra, 0))

    sibling = (kb, vir + 1 - 2 * core)
    rnext = dev(xx, f, (l + 1) & 7)
    lnext = dev(xx, f, (l + 7) & 7)

    low = pl.multiple_of(jnp.minimum((10 * vir >> 4) << 4, 128), 16)
    loads = [
        pltpu.make_async_copy(fold_any.at[:, :, pl.ds(low, 32)], fold, s0.at[0]),
        pltpu.make_async_copy(pair_any, pair, s0.at[1]),
        pltpu.make_async_copy(amps_any, amps.at[0], s0.at[2]),
        pltpu.make_async_copy(occt_any, occt, s0.at[3]),
        pltpu.make_async_copy(evir_any, evir, s0.at[4]),
    ]
    for c in loads:
        c.start()

    barrier = pltpu.get_barrier_semaphore()

    def greet(d):
        pl.semaphore_signal(barrier, inc=1, device_id=d, device_id_type=MESH)

    @pl.when(holds == 1)
    def _():
        greet(((kb + 16) & 31, vir))

        @pl.loop(1, 32)
        def _(i):
            @pl.when(i != 16)
            def _():
                greet(((kb + 16 + i) & 31, vir))

    @pl.loop(0, UNITS)
    def _(u):
        a, b = source(u)

        @pl.when((a != xx) | (b != f))
        def _():
            greet(dev(a, b, l))

    greet(rnext)
    greet(lnext)
    greet(sibling)

    pick = onehot(
        (iota((160, 512), 0) % 16 == iota((160, 512), 1) // 32)
        & (iota((160, 512), 1) % 32 + low == 10 * vir + iota((160, 512), 0) // 16)
    )
    row, col = iota((160, 128), 0), iota((160, 128), 1)
    tail = [onehot((row - 128 == col - 32 * j) & (row >= 128)) for j in range(4)]
    dot = functools.partial(jnp.dot, preferred_element_type=F32)
    loads[0].wait()
    loads[1].wait()
    rem = None
    for s in range(STEPS):
        at = plan[s] % 2
        p = pair[at]
        g = dot(pick, fold[at].reshape(512, 160)).astype(BF16)
        x[:, 2 * s] = p[:, :, :128]
        x[:, 2 * s + 1] = g[:, :128].reshape(10, 16, 128)
        ends = dot(p.reshape(160, 160), tail[2 * s]) + dot(g, tail[2 * s + 1])
        rem = ends if rem is None else rem + ends
    x[:, 4] = rem.astype(BF16).reshape(10, 16, 128)
    loads[2].wait()

    pl.semaphore_wait(barrier, UNITS - holds + 31 * holds + 2 + 1)

    def remote(src, dst, ss, rs, d):
        return pltpu.make_async_remote_copy(
            src_ref=src, dst_ref=dst, send_sem=ss, recv_sem=rs, device_id=d, device_id_type=MESH)

    def copy1(t, to, origin):
        return remote(x.at[t], cand.at[origin], s1.at[t], r1.at[origin], (to, vir))

    @pl.loop(0, UNITS)
    def _(t):
        to = holder(t)

        @pl.when(to != kb)
        def _():
            copy1(t, to, kb).start()

    swap = remote(amps.at[0], amps.at[1], s3.at[0], r3.at[0], sibling)
    swap.start()

    loads[3].wait()
    loads[4].wait()
    row, band = iota((128, 16), 0), iota((128, 16), 1)
    member = jnp.zeros((128, 16), jnp.bool_)
    start = 0
    for i in range(16):
        inside = (row >= start) & (row < start + 15 - i)
        member = member | (inside & ((band == i) | (band == i + 1 + row - start)))
        start += 15 - i
    exact = dict(precision=lax.Precision.HIGHEST, preferred_element_type=F32)
    sums = jnp.dot(jnp.where(member, 1.0, 0.0), occt[...], **exact)
    pe = jnp.sum(jnp.where(iota((128, 64), 1) == kfirst, sums, 0.0), axis=1, keepdims=True)
    level = iota((64, 160), 0)
    vrow = jnp.sum(jnp.where(level == kfirst, evir[...], 0.0), axis=0, keepdims=True)
    for who in range(2):
        owner = vir + who * (1 - 2 * core)
        for a in range(10):
            mine = jnp.sum(jnp.where(iota((1, 160), 1) == 10 * owner + a, vrow, 0.0), axis=1, keepdims=True)
            left[who, a] = jnp.broadcast_to(mine - pe, (128, 128))
    lane = iota((160, 128), 1)
    w = lane // 16
    v16 = jnp.where(flip, (w % 4 * 2 + w // 4) * 2 + 1, 2 * w)
    spread = jnp.where(iota((160, 128), 0) // 10 == v16, 1.0, 0.0)
    occ16 = lax.dot_general(
        occt[...], jnp.where(iota((16, 128), 1) % 16 == iota((16, 128), 0), 1.0, 0.0), TN, **exact)
    half = iota((1, 128), 1) < 64
    for s in range(STEPS):
        k3 = plan[s]
        k2 = kcons[kfirst, k3]
        vs = jnp.sum(jnp.where(level == k2, evir[...], 0.0), axis=0, keepdims=True)
        own = jnp.where(iota((16, 160), 1) % 10 == iota((16, 160), 0), vs, 0.0)
        occ = jnp.sum(jnp.where(iota((64, 128), 0) == k3, occ16, 0.0), axis=0, keepdims=True)
        table = jnp.dot(own, spread, **exact) - occ
        turned = pltpu.roll(table, 64, 1)
        for o in range(8):
            t = 2 * (o % 4)
            if o < 4:
                both = jnp.where(half, table[t:t + 1], turned[t + 1:t + 2])
            else:
                both = jnp.where(half, turned[t:t + 1], table[t + 1:t + 2])
            right[s, o:o + 1, :] = jnp.where(flip, both, table[o:o + 1])
        right[s, 8:10, :] = table[8:10]

    e, to = iota((160, 256), 0), iota((160, 256), 1)
    places = [onehot(e + jnp.where(e >= 128, 64 * s, 0) == to) for s in range(STEPS)]

    def lay(who):
        for s in range(STEPS):
            for a in range(10):
                rows[s, who, a, :120] = lax.dot_general(
                    amps[who, a], places[s], TN, preferred_element_type=F32).astype(BF16)
                rows[s, who, a, 120:] = jnp.zeros((8, 256), BF16)

    lay(0)

    @pl.when(holds == 1)
    def _():
        cand[kb] = x[column]

        @pl.loop(1, 32)
        def _(i):
            origin = (kb + i) & 31
            copy1(0, kb, origin).wait_recv()

        first, second = plan[0] // 2, plan[1] // 2
        buf[l, slot, 0] = cand[first, 0]
        buf[l, slot, 1] = cand[first, 1]
        buf[l, slot, 2] = cand[second, 2]
        buf[l, slot, 3] = cand[second, 3]
        buf[l, slot, 4] = jnp.where(
            iota((16, 128), 1) < 64, cand[first, 4].astype(F32), cand[second, 4].astype(F32)).astype(BF16)

    def copy2(i, u):
        here = buf.at[l, u]
        return remote(here, here, s2.at[i], r2.at[u], dev((xx + (i >> 3)) & 3, (f + i) & 7, l))

    @pl.when(holds == 1)
    def _():
        @pl.loop(1, 32)
        def _(i):
            copy2(i, slot).start()

    swap.wait_recv()
    lay(1)

    @pl.loop(0, UNITS)
    def _(u):
        a, b = source(u)

        @pl.when((a != xx) | (b != f))
        def _():
            copy2(1, u).wait_recv()

    def copy4(t, way, part, origin):
        here = buf.at[origin, pl.ds(5 * part, 5)]
        return remote(here, here, s4.at[t, way, part], r4.at[t, way, part], lnext if way else rnext)

    def chunk(n, places_of, edge):
        for s in range(STEPS):
            for i, (o, u) in enumerate(places_of):
                at = slice(16 * i, 16 * i + 16)
                pq[n % 2, s, at, :128] = buf[o, u, 2 * s]
                fq[n % 2, s, at, :128] = buf[o, u, 2 * s + 1]
                pq[n % 2, s, at, 128:] = buf[o, u, 4]
                fq[n % 2, s, at, 128:] = buf[o, u, 4]
        for s in range(STEPS):
            ends = edge(s)
            for m in (2, 3, 0, 1):
                mine = rows[s, m // 2, m % 2 * 5:m % 2 * 5 + 5].reshape(640, 256)
                lf = left[m // 2, m % 2 * 5:m % 2 * 5 + 5].reshape(640, 128)
                zeta = lax.dot_general(mine, pq[n % 2, s], NT, preferred_element_type=F32)
                tri = jnp.concatenate(
                    [(zeta[:, 128 * i:128 * i + 128] / (lf + ends[i])).astype(BF16) for i in range(2)], axis=1)
                got = jnp.dot(tri, fq[n % 2, s], preferred_element_type=F32)
                if n == 0:
                    acc[s, m] = got
                else:
                    acc[s, m] += got

    def pair_of(o1, o2):
        return [(o, u) for o in (o1, o2) for u in range(8)], lambda s: [right[s, pl.ds(o, 1), :] for o in (o1, o2)]

    for part in range(2):
        for way in range(2):
            copy4(0, way, part, l).start()
    for t in range(1, 5):
        for part in range(2):
            for way in range(2):
                if t == 4 and way != part:
                    continue
                origin = (l + t) & 7 if way else (l + 8 - t) & 7
                copy4(t - 1, way, part, origin).wait_recv()
                if t < 3 or (t == 3 and way == part):
                    copy4(t, way, part, origin).start()
        if t < 4:
            chunk(t - 1, *pair_of((l + 8 - t) & 7, (l + t) & 7))
    chunk(3, *pair_of(l, (l + 4) & 7))
    chunk(4, [(o, u) for u in (8, 9) for o in range(8)], lambda s: [right[s, 8:9, :], right[s, 9:10, :]])

    row = iota((160, 256), 0)
    back = onehot(row + jnp.where(row >= 128, 32, 0) == iota((160, 256), 1))

    def turn(m):
        even, odd = acc[0, m], acc[1, m]
        total = jnp.concatenate(
            [even[:, :128] + odd[:, :128], even[:, 128:] + pltpu.roll(odd[:, 128:], 64, 1)], axis=1)
        high = total.astype(BF16)
        rest = (total - high.astype(F32)).astype(BF16)
        return [lax.dot_general(back, h, NT, preferred_element_type=F32) for h in (high, rest)]

    def copy5(m):
        return remote(part_out.at[m], part_in.at[m], s5.at[m], r5.at[m], sibling)

    for m in range(2):
        high, rest = turn(2 + m)
        part_out[m, 0] = high.astype(BF16)
        part_out[m, 1] = rest.astype(BF16)
        copy5(m).start()
    for m in range(2):
        high, rest = turn(m)
        copy5(m).wait_recv()
        done = (high + part_in[m, 0].astype(F32) + (rest + part_in[m, 1].astype(F32))).astype(BF16)
        for a in range(5):
            out[5 * m + a] = done[:, 128 * a:128 * a + 120]

    @pl.loop(0, UNITS)
    def _(t):
        to = holder(t)

        @pl.when(to != kb)
        def _():
            copy1(t, to, kb).wait_send()

    @pl.when(holds == 1)
    def _():
        @pl.loop(1, 32)
        def _(i):
            copy2(i, slot).wait_send()

    swap.wait_send()
    for t in range(4):
        for part in range(2):
            for way in range(2):
                if t == 3 and way != part:
                    continue
                origin = (l + t) & 7 if way else (l + 8 - t) & 7
                copy4(t, way, part, origin).wait_send()
    for m in range(2):
        copy5(m).wait_send()


def local(amps, ints_pair, ints_fold, eps_occ, eps_vir, kconserve, plan):
    smem = pl.BlockSpec(memory_space=pltpu.SMEM)
    anywhere = pl.BlockSpec(memory_space=pl.ANY)
    dma = pltpu.SemaphoreType.DMA
    out = pl.pallas_call(
        kernel,
        out_shape=jax.ShapeDtypeStruct((10, 160, 120), BF16),
        in_specs=[smem, smem] + [anywhere] * 5,
        out_specs=pl.BlockSpec(memory_space=pltpu.VMEM),
        scratch_shapes=[
            pltpu.VMEM((2, 10, 160, 120), BF16),
            pltpu.VMEM((2, 10, 16, 160), BF16),
            pltpu.VMEM((2, 16, 32, 160), BF16),
            pltpu.VMEM((16, 64), F32),
            pltpu.VMEM((64, 160), F32),
            pltpu.VMEM((UNITS, 5, 16, 128), BF16),
            pltpu.VMEM((2, 2, 10, 128, 256), BF16),
            pltpu.VMEM((2, 10, 128, 128), F32),
            pltpu.VMEM((2, 16, 128), F32),
            pltpu.VMEM((32, 5, 16, 128), BF16),
            pltpu.VMEM((8, UNITS, 5, 16, 128), BF16),
            pltpu.VMEM((2, 2, 256, 256), BF16),
            pltpu.VMEM((2, 2, 256, 256), BF16),
            pltpu.VMEM((2, 4, 640, 256), F32),
            pltpu.VMEM((2, 2, 160, 640), BF16),
            pltpu.VMEM((2, 2, 160, 640), BF16),
            dma((5,)),
            dma((UNITS,)), dma((32,)),
            dma((32,)), dma((UNITS,)),
            dma((1,)), dma((1,)),
            dma((4, 2, 2)), dma((4, 2, 2)),
            dma((2,)), dma((2,)),
        ],
        compiler_params=pltpu.CompilerParams(
            vmem_limit_bytes=56 * 2**20, collective_id=0, has_side_effects=True),
        name="triples",
    )(plan, kconserve, jnp.transpose(amps, (0, 2, 3, 1))[0], jnp.transpose(ints_pair, (0, 3, 2, 1)),
      ints_fold, eps_occ.T, eps_vir)
    return jnp.transpose(out, (2, 0, 1))[None]


def solution(mesh):
    return jax.shard_map(
        local,
        mesh=mesh,
        in_specs=(
            P("kb", None, "vir", None),
            P("kb", None, None, "vir"),
            P("kb", None, None, None),
            P(),
            P(),
            P(),
            P(),
        ),
        out_specs=P("kb", None, "vir", None),
        check_vma=False,
    )
```

```python
import functools

import jax
import jax.numpy as jnp
import numpy as np
from jax import lax
from jax.experimental import pallas as pl
from jax.experimental.pallas import tpu as pltpu
from jax.sharding import PartitionSpec as P

STEPS = 2
UNITS = 10
MESH = pl.DeviceIdType.MESH
F32 = jnp.float32
BF16 = jnp.bfloat16
NT = (((1,), (1,)), ((), ()))
TN = (((0,), (0,)), ((), ()))


def iota(shape, dim):
    return lax.broadcasted_iota(jnp.int32, shape, dim)


def onehot(mask):
    return jnp.where(mask, 1.0, 0.0).astype(BF16)


def kernel(plan, kcons, amps_any, pair_any, fold_any, occt_any, evir_any, out,
           amps, pair, fold, occt, evir, x, rows, left, right, cand, buf, pq, fq, acc, part_out, part_in,
           mid, got, s0, s1, r1, s2, r2, s3, r3, s4, r4, s5, r5, s6, r6, s7, r7):
    kb = lax.axis_index("kb")
    vir = lax.axis_index("vir")
    z, yl = kb >> 2, kb & 3
    xx, yh, core = vir >> 2, (vir >> 1) & 1, vir & 1
    y = yh * 4 + yl
    flip = core == 1
    f = jnp.where(flip, z, y)
    l = jnp.where(flip, y, z)
    kfirst = 2 * kb

    def dev(x_, f_, l_):
        y_ = jnp.where(flip, l_, f_)
        z_ = jnp.where(flip, f_, l_)
        return (z_ * 4 + (y_ & 3), x_ * 4 + (y_ >> 2) * 2 + core)

    def holder(t):
        v8 = xx * 2 + yh
        last = t >= 8
        z0 = jnp.where(last, v8, t)
        y0 = (z0 + xx + jnp.where(last, t - 7, 0)) & 3
        z1 = jnp.where(last, (xx + 4 * t - 30) & 7, (t & 1) * 4 + xx)
        y1 = jnp.where(last, xx, t >> 1)
        return jnp.where(flip, z1, z0), jnp.where(flip, y1, y0)

    def source(u):
        last = u >= 8
        v8 = jnp.where(last, l, u)
        y0 = (v8 & 1) * 4 + ((l + (v8 >> 1) + jnp.where(last, u - 7, 0)) & 3)
        ll = l & 3
        x1 = jnp.where(last, ll, u & 3)
        z1 = jnp.where(last, (ll + 4 * u - 30) & 7, u)
        return jnp.where(flip, x1, v8 >> 1), jnp.where(flip, z1, y0)

    sibling = (kb, vir + 1 - 2 * core)
    rnext = dev(xx, f, (l + 1) & 7)
    lnext = dev(xx, f, (l + 7) & 7)

    low = pl.multiple_of(jnp.minimum((10 * vir >> 4) << 4, 128), 16)
    loads = [
        pltpu.make_async_copy(fold_any.at[:, :, pl.ds(low, 32)], fold, s0.at[0]),
        pltpu.make_async_copy(pair_any, pair, s0.at[1]),
        pltpu.make_async_copy(amps_any, amps.at[0], s0.at[2]),
        pltpu.make_async_copy(occt_any, occt, s0.at[3]),
        pltpu.make_async_copy(evir_any, evir, s0.at[4]),
    ]
    for c in loads:
        c.start()

    barrier = pltpu.get_barrier_semaphore()

    def far(i):
        step = (i + 1) >> 1
        return 4 - jnp.where((i & 1) == 1, step, -step)

    def greet(d):
        pl.semaphore_signal(barrier, inc=1, device_id=d, device_id_type=MESH)

    @pl.loop(1, 4)
    def _(i):
        greet((z * 4 + ((yl + i) & 3), vir))

    @pl.loop(0, 7)
    def _(i):
        greet((((z + far(i)) & 7) * 4 + yl, vir))

    @pl.loop(1, 4)
    def _(i):
        greet(dev((xx + i) & 3, f, l))

    @pl.loop(0, 7)
    def _(i):
        greet(dev(xx, (f + far(i)) & 7, l))

    greet(rnext)
    greet(lnext)
    greet(sibling)

    pick = onehot(
        (iota((160, 512), 0) % 16 == iota((160, 512), 1) // 32)
        & (iota((160, 512), 1) % 32 + low == 10 * vir + iota((160, 512), 0) // 16)
    )
    row, col = iota((160, 128), 0), iota((160, 128), 1)
    tail = [onehot((row - 128 == col - 32 * j) & (row >= 128)) for j in range(4)]
    dot = functools.partial(jnp.dot, preferred_element_type=F32)
    loads[0].wait()
    loads[1].wait()
    rem = None
    for s in range(STEPS):
        at = plan[s] % 2
        p = pair[at]
        g = dot(pick, fold[at].reshape(512, 160)).astype(BF16)
        x[:, 2 * s] = p[:, :, :128]
        x[:, 2 * s + 1] = g[:, :128].reshape(10, 16, 128)
        ends = dot(p.reshape(160, 160), tail[2 * s]) + dot(g, tail[2 * s + 1])
        rem = ends if rem is None else rem + ends
    x[:, 4] = rem.astype(BF16).reshape(10, 16, 128)
    loads[2].wait()

    pl.semaphore_wait(barrier, 3 + 7 + 3 + 7 + 2 + 1)

    def remote(src, dst, ss, rs, d):
        return pltpu.make_async_remote_copy(
            src_ref=src, dst_ref=dst, send_sem=ss, recv_sem=rs, device_id=d, device_id_type=MESH)

    def copy1(t, there):
        return remote(x.at[t], cand.at[yl, t], s1.at[t], r1.at[yl, t], (z * 4 + there, vir))

    @pl.loop(0, UNITS)
    def _(t):
        there = holder(t)[1]

        @pl.when(there != yl)
        def _():
            copy1(t, there).start()

        @pl.when(there == yl)
        def _():
            cand[yl, t] = x[t]

    swap = remote(amps.at[0], amps.at[1], s3.at[0], r3.at[0], sibling)
    swap.start()

    loads[3].wait()
    loads[4].wait()
    row, band = iota((128, 16), 0), iota((128, 16), 1)
    member = jnp.zeros((128, 16), jnp.bool_)
    start = 0
    for i in range(16):
        inside = (row >= start) & (row < start + 15 - i)
        member = member | (inside & ((band == i) | (band == i + 1 + row - start)))
        start += 15 - i
    exact = dict(precision=lax.Precision.HIGHEST, preferred_element_type=F32)
    sums = jnp.dot(jnp.where(member, 1.0, 0.0), occt[...], **exact)
    pe = jnp.sum(jnp.where(iota((128, 64), 1) == kfirst, sums, 0.0), axis=1, keepdims=True)
    level = iota((64, 160), 0)
    vrow = jnp.sum(jnp.where(level == kfirst, evir[...], 0.0), axis=0, keepdims=True)
    for who in range(2):
        owner = vir + who * (1 - 2 * core)
        for a in range(10):
            mine = jnp.sum(jnp.where(iota((1, 160), 1) == 10 * owner + a, vrow, 0.0), axis=1, keepdims=True)
            left[who, a] = jnp.broadcast_to(mine - pe, (128, 128))
    lane = iota((160, 128), 1)
    w = lane // 16
    v16 = jnp.where(flip, (w % 4 * 2 + w // 4) * 2 + 1, 2 * w)
    spread = jnp.where(iota((160, 128), 0) // 10 == v16, 1.0, 0.0)
    occ16 = lax.dot_general(
        occt[...], jnp.where(iota((16, 128), 1) % 16 == iota((16, 128), 0), 1.0, 0.0), TN, **exact)
    half = iota((1, 128), 1) < 64
    for s in range(STEPS):
        k3 = plan[s]
        k2 = kcons[kfirst, k3]
        vs = jnp.sum(jnp.where(level == k2, evir[...], 0.0), axis=0, keepdims=True)
        own = jnp.where(iota((16, 160), 1) % 10 == iota((16, 160), 0), vs, 0.0)
        occ = jnp.sum(jnp.where(iota((64, 128), 0) == k3, occ16, 0.0), axis=0, keepdims=True)
        table = jnp.dot(own, spread, **exact) - occ
        turned = pltpu.roll(table, 64, 1)
        for o in range(8):
            t = 2 * (o % 4)
            if o < 4:
                both = jnp.where(half, table[t:t + 1], turned[t + 1:t + 2])
            else:
                both = jnp.where(half, turned[t:t + 1], table[t + 1:t + 2])
            right[s, o:o + 1, :] = jnp.where(flip, both, table[o:o + 1])
        right[s, 8:10, :] = table[8:10]

    e, to = iota((160, 256), 0), iota((160, 256), 1)
    places = [onehot(e + jnp.where(e >= 128, 64 * s, 0) == to) for s in range(STEPS)]

    def lay(who):
        for s in range(STEPS):
            for a in range(10):
                rows[s, who, a, :120] = lax.dot_general(
                    amps[who, a], places[s], TN, preferred_element_type=F32).astype(BF16)
                rows[s, who, a, 120:] = jnp.zeros((8, 256), BF16)

    first, second = plan[0] // 2, plan[1] // 2
    split = iota((16, 128), 1) < 64

    def copy2(t, there):
        return remote(mid.at[t], got.at[z, t], s2.at[t], r2.at[z, t], (there * 4 + yl, vir))

    @pl.loop(0, UNITS)
    def _(t):
        @pl.when(holder(t)[1] == yl)
        def _():
            @pl.loop(1, 4)
            def _(i):
                other = (yl + i) & 3
                remote(x.at[t], cand.at[other, t], s1.at[t], r1.at[other, t], (z * 4 + yl, vir)).wait_recv()

    @pl.loop(0, UNITS)
    def _(t):
        there, row_ = holder(t)

        @pl.when(row_ == yl)
        def _():
            one, two = first & 3, second & 3
            mid[t, 0] = cand[one, t, 0]
            mid[t, 1] = cand[one, t, 1]
            mid[t, 2] = cand[two, t, 2]
            mid[t, 3] = cand[two, t, 3]
            mid[t, 4] = jnp.where(split, cand[one, t, 4].astype(F32), cand[two, t, 4].astype(F32)).astype(BF16)

            @pl.when(there != z)
            def _():
                copy2(t, there).start()

            @pl.when(there == z)
            def _():
                got[z, t] = mid[t]

    lay(0)

    def slot_of(t):
        u0 = jnp.where(t >= 8, t, xx * 2 + yh)
        u1 = jnp.where(t >= 8, t, (t & 1) * 4 + xx)
        return jnp.where(flip, u1, u0)

    def copy3(u, i):
        here = buf.at[l, u]
        return remote(here, here, s6.at[i, u], r6.at[u], dev((xx + i) & 3, f, l))

    @pl.loop(0, UNITS)
    def _(t):
        there, row_ = holder(t)

        @pl.when((row_ == yl) & (there == z))
        def _():
            @pl.loop(1, 8)
            def _(i):
                other = (z + i) & 7
                remote(mid.at[t], got.at[other, t], s2.at[t], r2.at[other, t], (z * 4 + yl, vir)).wait_recv()

            one, two = first >> 2, second >> 2
            u = slot_of(t)
            buf[l, u, 0] = got[one, t, 0]
            buf[l, u, 1] = got[one, t, 1]
            buf[l, u, 2] = got[two, t, 2]
            buf[l, u, 3] = got[two, t, 3]
            buf[l, u, 4] = jnp.where(split, got[one, t, 4].astype(F32), got[two, t, 4].astype(F32)).astype(BF16)

            @pl.loop(1, 4)
            def _(i):
                copy3(u, 4 - i).start()

    def copy6(u, i):
        here = buf.at[l, u]
        return remote(here, here, s7.at[i, u], r7.at[u], dev(xx, (f + i) & 7, l))

    @pl.loop(0, UNITS)
    def _(u):
        a, b = source(u)

        @pl.when(b == f)
        def _():
            @pl.when(a != xx)
            def _():
                copy3(u, 1).wait_recv()

            @pl.loop(0, 7)
            def _(i):
                copy6(u, far(i)).start()

    swap.wait_recv()
    lay(1)

    @pl.loop(0, UNITS)
    def _(u):
        @pl.when(source(u)[1] != f)
        def _():
            copy6(u, 1).wait_recv()

    def copy4(t, way, part, origin):
        here = buf.at[origin, pl.ds(5 * part, 5)]
        return remote(here, here, s4.at[t, way, part], r4.at[t, way, part], lnext if way else rnext)

    row = iota((160, 256), 0)
    back = onehot(row + jnp.where(row >= 128, 32, 0) == iota((160, 256), 1))

    def turn(m):
        even, odd = acc[0, m], acc[1, m]
        total = jnp.concatenate(
            [even[:, :128] + odd[:, :128], even[:, 128:] + pltpu.roll(odd[:, 128:], 64, 1)], axis=1)
        high = total.astype(BF16)
        rest = (total - high.astype(F32)).astype(BF16)
        return [lax.dot_general(back, h, NT, preferred_element_type=F32) for h in (high, rest)]

    def copy5(m):
        return remote(part_out.at[m], part_in.at[m], s5.at[m], r5.at[m], sibling)

    def hand_over():
        for m in range(2):
            high, rest = turn(2 + m)
            part_out[m, 0] = high.astype(BF16)
            part_out[m, 1] = rest.astype(BF16)
            copy5(m).start()

    def chunk(n, places_of, edge):
        for s in range(STEPS):
            for i, (o, u) in enumerate(places_of):
                at = slice(16 * i, 16 * i + 16)
                pq[n % 2, s, at, :128] = buf[o, u, 2 * s]
                fq[n % 2, s, at, :128] = buf[o, u, 2 * s + 1]
                pq[n % 2, s, at, 128:] = buf[o, u, 4]
                fq[n % 2, s, at, 128:] = buf[o, u, 4]
        for ms in ((2, 3), (0, 1)):
            for s in range(STEPS):
                ends = edge(s)
                for m in ms:
                    mine = rows[s, m // 2, m % 2 * 5:m % 2 * 5 + 5].reshape(640, 256)
                    lf = left[m // 2, m % 2 * 5:m % 2 * 5 + 5].reshape(640, 128)
                    zeta = lax.dot_general(mine, pq[n % 2, s], NT, preferred_element_type=F32)
                    tri = jnp.concatenate(
                        [(zeta[:, 128 * i:128 * i + 128] / (lf + ends[i])).astype(BF16) for i in range(2)], axis=1)
                    term = jnp.dot(tri, fq[n % 2, s], preferred_element_type=F32)
                    if n == 0:
                        acc[s, m] = term
                    else:
                        acc[s, m] += term
            if n == 4 and ms[0] == 2:
                hand_over()

    def pair_of(o1, o2):
        return [(o, u) for o in (o1, o2) for u in range(8)], lambda s: [right[s, pl.ds(o, 1), :] for o in (o1, o2)]

    for part in range(2):
        for way in range(2):
            copy4(0, way, part, l).start()
    for t in range(1, 5):
        for part in range(2):
            for way in range(2):
                if t == 4 and way != part:
                    continue
                origin = (l + t) & 7 if way else (l + 8 - t) & 7
                copy4(t - 1, way, part, origin).wait_recv()
                if t < 3 or (t == 3 and way == part):
                    copy4(t, way, part, origin).start()
        if t < 4:
            chunk(t - 1, *pair_of((l + 8 - t) & 7, (l + t) & 7))
    chunk(3, *pair_of(l, (l + 4) & 7))
    chunk(4, [(o, u) for u in (8, 9) for o in range(8)], lambda s: [right[s, 8:9, :], right[s, 9:10, :]])

    for m in range(2):
        high, rest = turn(m)
        copy5(m).wait_recv()
        done = (high + part_in[m, 0].astype(F32) + (rest + part_in[m, 1].astype(F32))).astype(BF16)
        for a in range(5):
            out[5 * m + a] = done[:, 128 * a:128 * a + 120]

    @pl.loop(0, UNITS)
    def _(t):
        there, row_ = holder(t)

        @pl.when(row_ != yl)
        def _():
            copy1(t, row_).wait_send()

        @pl.when((row_ == yl) & (there != z))
        def _():
            copy2(t, there).wait_send()

        @pl.when((row_ == yl) & (there == z))
        def _():
            @pl.loop(1, 4)
            def _(i):
                copy3(slot_of(t), i).wait_send()

        @pl.when(source(t)[1] == f)
        def _():
            @pl.loop(1, 8)
            def _(i):
                copy6(t, i).wait_send()

    swap.wait_send()
    for t in range(4):
        for part in range(2):
            for way in range(2):
                if t == 3 and way != part:
                    continue
                origin = (l + t) & 7 if way else (l + 8 - t) & 7
                copy4(t, way, part, origin).wait_send()
    for m in range(2):
        copy5(m).wait_send()


def local(amps, ints_pair, ints_fold, eps_occ, eps_vir, kconserve, plan):
    smem = pl.BlockSpec(memory_space=pltpu.SMEM)
    anywhere = pl.BlockSpec(memory_space=pl.ANY)
    dma = pltpu.SemaphoreType.DMA
    out = pl.pallas_call(
        kernel,
        out_shape=jax.ShapeDtypeStruct((10, 160, 120), BF16),
        in_specs=[smem, smem] + [anywhere] * 5,
        out_specs=pl.BlockSpec(memory_space=pltpu.VMEM),
        scratch_shapes=[
            pltpu.VMEM((2, 10, 160, 120), BF16),
            pltpu.VMEM((2, 10, 16, 160), BF16),
            pltpu.VMEM((2, 16, 32, 160), BF16),
            pltpu.VMEM((16, 64), F32),
            pltpu.VMEM((64, 160), F32),
            pltpu.VMEM((UNITS, 5, 16, 128), BF16),
            pltpu.VMEM((2, 2, 10, 128, 256), BF16),
            pltpu.VMEM((2, 10, 128, 128), F32),
            pltpu.VMEM((2, 16, 128), F32),
            pltpu.VMEM((4, UNITS, 5, 16, 128), BF16),
            pltpu.VMEM((8, UNITS, 5, 16, 128), BF16),
            pltpu.VMEM((2, 2, 256, 256), BF16),
            pltpu.VMEM((2, 2, 256, 256), BF16),
            pltpu.VMEM((2, 4, 640, 256), F32),
            pltpu.VMEM((2, 2, 160, 640), BF16),
            pltpu.VMEM((2, 2, 160, 640), BF16),
            pltpu.VMEM((UNITS, 5, 16, 128), BF16),
            pltpu.VMEM((8, UNITS, 5, 16, 128), BF16),
            dma((5,)),
            dma((UNITS,)), dma((4, UNITS)),
            dma((UNITS,)), dma((8, UNITS)),
            dma((1,)), dma((1,)),
            dma((4, 2, 2)), dma((4, 2, 2)),
            dma((2,)), dma((2,)),
            dma((4, UNITS)), dma((UNITS,)),
            dma((8, UNITS)), dma((UNITS,)),
        ],
        compiler_params=pltpu.CompilerParams(
            vmem_limit_bytes=56 * 2**20, collective_id=0, has_side_effects=True),
        name="triples",
    )(plan, kconserve, jnp.transpose(amps, (0, 2, 3, 1))[0], jnp.transpose(ints_pair, (0, 3, 2, 1)),
      ints_fold, eps_occ.T, eps_vir)
    return jnp.transpose(out, (2, 0, 1))[None]


def solution(mesh):
    return jax.shard_map(
        local,
        mesh=mesh,
        in_specs=(
            P("kb", None, "vir", None),
            P("kb", None, None, "vir"),
            P("kb", None, None, None),
            P(),
            P(),
            P(),
            P(),
        ),
        out_specs=P("kb", None, "vir", None),
        check_vma=False,
    )
```

```python
import functools

import jax
import jax.numpy as jnp
import numpy as np
from jax import lax
from jax.experimental import pallas as pl
from jax.experimental.pallas import tpu as pltpu
from jax.sharding import PartitionSpec as P

STEPS = 2
UNITS = 10
MESH = pl.DeviceIdType.MESH
F32 = jnp.float32
BF16 = jnp.bfloat16
NT = (((1,), (1,)), ((), ()))
TN = (((0,), (0,)), ((), ()))


def iota(shape, dim):
    return lax.broadcasted_iota(jnp.int32, shape, dim)


def onehot(mask):
    return jnp.where(mask, 1.0, 0.0).astype(BF16)


def kernel(plan_any, kcons_any, amps_any, pair_any, fold_any, occt_any, evir_any, out,
           plan, kcons, amps, pair, fold, occt, evir, x, rows, left, right, cand, buf, pq, fq, acc, part_out, part_in,
           mid, got, s0, s1, r1, s2, r2, s3, r3, s4, r4, s5, r5, s6, r6, s7, r7):
    kb = lax.axis_index("kb")
    vir = lax.axis_index("vir")
    z, yl = kb >> 2, kb & 3
    xx, yh, core = vir >> 2, (vir >> 1) & 1, vir & 1
    y = yh * 4 + yl
    flip = core == 1
    f = jnp.where(flip, z, y)
    l = jnp.where(flip, y, z)
    kfirst = 2 * kb

    def dev(x_, f_, l_):
        y_ = jnp.where(flip, l_, f_)
        z_ = jnp.where(flip, f_, l_)
        return (z_ * 4 + (y_ & 3), x_ * 4 + (y_ >> 2) * 2 + core)

    def holder(t):
        v8 = xx * 2 + yh
        last = t >= 8
        z0 = jnp.where(last, v8, t)
        y0 = (z0 + xx + jnp.where(last, t - 7, 0)) & 3
        z1 = jnp.where(last, (xx + 4 * t - 30) & 7, (t & 1) * 4 + xx)
        y1 = jnp.where(last, xx, t >> 1)
        return jnp.where(flip, z1, z0), jnp.where(flip, y1, y0)

    def source(u):
        last = u >= 8
        v8 = jnp.where(last, l, u)
        y0 = (v8 & 1) * 4 + ((l + (v8 >> 1) + jnp.where(last, u - 7, 0)) & 3)
        ll = l & 3
        x1 = jnp.where(last, ll, u & 3)
        z1 = jnp.where(last, (ll + 4 * u - 30) & 7, u)
        return jnp.where(flip, x1, v8 >> 1), jnp.where(flip, z1, y0)

    sibling = (kb, vir + 1 - 2 * core)
    rnext = dev(xx, f, (l + 1) & 7)
    lnext = dev(xx, f, (l + 7) & 7)

    low = pl.multiple_of(jnp.minimum((10 * vir >> 4) << 4, 128), 16)
    loads = [
        pltpu.make_async_copy(fold_any.at[:, :, pl.ds(low, 32)], fold, s0.at[0]),
        pltpu.make_async_copy(pair_any, pair, s0.at[1]),
        pltpu.make_async_copy(amps_any, amps.at[0], s0.at[2]),
        pltpu.make_async_copy(occt_any, occt, s0.at[3]),
        pltpu.make_async_copy(evir_any, evir, s0.at[4]),
        pltpu.make_async_copy(kcons_any, kcons, s0.at[5]),
        pltpu.make_async_copy(plan_any, plan, s0.at[6]),
    ]
    for c in loads:
        c.start()

    barrier = pltpu.get_barrier_semaphore()

    def far(i):
        step = (i + 1) >> 1
        return 4 - jnp.where((i & 1) == 1, step, -step)

    def greet(d):
        pl.semaphore_signal(barrier, inc=1, device_id=d, device_id_type=MESH)

    @pl.loop(0, 7)
    def _(i):
        greet((((z + far(i)) & 7) * 4 + yl, vir))
        greet(dev(xx, (f + far(i)) & 7, l))

    @pl.loop(1, 4)
    def _(i):
        greet((z * 4 + ((yl + i) & 3), vir))
        greet(dev((xx + i) & 3, f, l))

    greet(rnext)
    greet(lnext)
    greet(sibling)

    pick = onehot(
        (iota((160, 512), 0) % 16 == iota((160, 512), 1) // 32)
        & (iota((160, 512), 1) % 32 + low == 10 * vir + iota((160, 512), 0) // 16)
    )
    row, col = iota((160, 128), 0), iota((160, 128), 1)
    tail = [onehot((row - 128 == col - 32 * j) & (row >= 128)) for j in range(4)]
    dot = functools.partial(jnp.dot, preferred_element_type=F32)
    loads[6].wait()
    loads[0].wait()
    loads[1].wait()
    rem = None
    for s in range(STEPS):
        at = plan[s] % 2
        p = pair[at]
        g = dot(pick, fold[at].reshape(512, 160)).astype(BF16)
        x[:, 2 * s] = p[:, :, :128]
        x[:, 2 * s + 1] = g[:, :128].reshape(10, 16, 128)
        ends = dot(p.reshape(160, 160), tail[2 * s]) + dot(g, tail[2 * s + 1])
        rem = ends if rem is None else rem + ends
    x[:, 4] = rem.astype(BF16).reshape(10, 16, 128)
    loads[2].wait()

    pl.semaphore_wait(barrier, 3 + 7 + 3 + 7 + 2 + 1)

    def remote(src, dst, ss, rs, d):
        return pltpu.make_async_remote_copy(
            src_ref=src, dst_ref=dst, send_sem=ss, recv_sem=rs, device_id=d, device_id_type=MESH)

    def copy1(t, there):
        return remote(x.at[t], cand.at[yl, t], s1.at[t], r1.at[yl, t], (z * 4 + there, vir))

    @pl.loop(0, UNITS)
    def _(t):
        there = holder(t)[1]

        @pl.when(there != yl)
        def _():
            copy1(t, there).start()

        @pl.when(there == yl)
        def _():
            cand[yl, t] = x[t]

    swap = remote(amps.at[0], amps.at[1], s3.at[0], r3.at[0], sibling)
    swap.start()

    loads[3].wait()
    loads[4].wait()
    loads[5].wait()
    row, band = iota((128, 16), 0), iota((128, 16), 1)
    member = jnp.zeros((128, 16), jnp.bool_)
    start = 0
    for i in range(16):
        inside = (row >= start) & (row < start + 15 - i)
        member = member | (inside & ((band == i) | (band == i + 1 + row - start)))
        start += 15 - i
    exact = dict(precision=lax.Precision.HIGHEST, preferred_element_type=F32)
    sums = jnp.dot(jnp.where(member, 1.0, 0.0), occt[...], **exact)
    pe = jnp.sum(jnp.where(iota((128, 64), 1) == kfirst, sums, 0.0), axis=1, keepdims=True)
    level = iota((64, 160), 0)
    vrow = jnp.sum(jnp.where(level == kfirst, evir[...], 0.0), axis=0, keepdims=True)
    for who in range(2):
        owner = vir + who * (1 - 2 * core)
        for a in range(10):
            mine = jnp.sum(jnp.where(iota((1, 160), 1) == 10 * owner + a, vrow, 0.0), axis=1, keepdims=True)
            left[who, a] = jnp.broadcast_to(mine - pe, (128, 128))
    lane = iota((160, 128), 1)
    w = lane // 16
    v16 = jnp.where(flip, (w % 4 * 2 + w // 4) * 2 + 1, 2 * w)
    spread = jnp.where(iota((160, 128), 0) // 10 == v16, 1.0, 0.0)
    occ16 = lax.dot_general(
        occt[...], jnp.where(iota((16, 128), 1) % 16 == iota((16, 128), 0), 1.0, 0.0), TN, **exact)
    half = iota((1, 128), 1) < 64
    for s in range(STEPS):
        k3 = plan[s]
        k2 = kcons[kfirst, k3]
        vs = jnp.sum(jnp.where(level == k2, evir[...], 0.0), axis=0, keepdims=True)
        own = jnp.where(iota((16, 160), 1) % 10 == iota((16, 160), 0), vs, 0.0)
        occ = jnp.sum(jnp.where(iota((64, 128), 0) == k3, occ16, 0.0), axis=0, keepdims=True)
        table = jnp.dot(own, spread, **exact) - occ
        turned = pltpu.roll(table, 64, 1)
        for o in range(8):
            t = 2 * (o % 4)
            if o < 4:
                both = jnp.where(half, table[t:t + 1], turned[t + 1:t + 2])
            else:
                both = jnp.where(half, turned[t:t + 1], table[t + 1:t + 2])
            right[s, o:o + 1, :] = jnp.where(flip, both, table[o:o + 1])
        right[s, 8:10, :] = table[8:10]

    e, to = iota((160, 256), 0), iota((160, 256), 1)
    places = [onehot(e + jnp.where(e >= 128, 64 * s, 0) == to) for s in range(STEPS)]

    def lay(who):
        for s in range(STEPS):
            for a in range(10):
                rows[s, who, a, :120] = lax.dot_general(
                    amps[who, a], places[s], TN, preferred_element_type=F32).astype(BF16)
                rows[s, who, a, 120:] = jnp.zeros((8, 256), BF16)

    first, second = plan[0] // 2, plan[1] // 2
    split = iota((16, 128), 1) < 64

    def copy2(t, there):
        return remote(mid.at[t], got.at[z, t], s2.at[t], r2.at[z, t], (there * 4 + yl, vir))

    @pl.loop(0, UNITS)
    def _(t):
        @pl.when(holder(t)[1] == yl)
        def _():
            @pl.loop(1, 4)
            def _(i):
                other = (yl + i) & 3
                remote(x.at[t], cand.at[other, t], s1.at[t], r1.at[other, t], (z * 4 + yl, vir)).wait_recv()

    @pl.loop(0, UNITS)
    def _(t):
        there, row_ = holder(t)

        @pl.when(row_ == yl)
        def _():
            one, two = first & 3, second & 3
            mid[t, 0] = cand[one, t, 0]
            mid[t, 1] = cand[one, t, 1]
            mid[t, 2] = cand[two, t, 2]
            mid[t, 3] = cand[two, t, 3]
            mid[t, 4] = jnp.where(split, cand[one, t, 4].astype(F32), cand[two, t, 4].astype(F32)).astype(BF16)

            @pl.when(there != z)
            def _():
                copy2(t, there).start()

            @pl.when(there == z)
            def _():
                got[z, t] = mid[t]

    lay(0)

    def slot_of(t):
        u0 = jnp.where(t >= 8, t, xx * 2 + yh)
        u1 = jnp.where(t >= 8, t, (t & 1) * 4 + xx)
        return jnp.where(flip, u1, u0)

    def copy3(u, i):
        here = buf.at[l, u]
        return remote(here, here, s6.at[i, u], r6.at[u], dev((xx + i) & 3, f, l))

    @pl.loop(0, UNITS)
    def _(t):
        there, row_ = holder(t)

        @pl.when((row_ == yl) & (there == z))
        def _():
            @pl.loop(1, 8)
            def _(i):
                other = (z + i) & 7
                remote(mid.at[t], got.at[other, t], s2.at[t], r2.at[other, t], (z * 4 + yl, vir)).wait_recv()

            one, two = first >> 2, second >> 2
            u = slot_of(t)
            buf[l, u, 0] = got[one, t, 0]
            buf[l, u, 1] = got[one, t, 1]
            buf[l, u, 2] = got[two, t, 2]
            buf[l, u, 3] = got[two, t, 3]
            buf[l, u, 4] = jnp.where(split, got[one, t, 4].astype(F32), got[two, t, 4].astype(F32)).astype(BF16)

            @pl.loop(1, 4)
            def _(i):
                copy3(u, 4 - i).start()

    def copy6(u, i):
        here = buf.at[l, u]
        return remote(here, here, s7.at[i, u], r7.at[u], dev(xx, (f + i) & 7, l))

    @pl.loop(0, UNITS)
    def _(u):
        a, b = source(u)

        @pl.when(b == f)
        def _():
            @pl.when(a != xx)
            def _():
                copy3(u, 1).wait_recv()

            @pl.loop(0, 7)
            def _(i):
                copy6(u, far(i)).start()

    swap.wait_recv()
    lay(1)

    @pl.loop(0, UNITS)
    def _(u):
        @pl.when(source(u)[1] != f)
        def _():
            copy6(u, 1).wait_recv()

    def copy4(t, way, part, origin):
        here = buf.at[origin, pl.ds(2 * part, 2)]
        return remote(here, here, s4.at[t, way, part], r4.at[t, way, part], lnext if way else rnext)

    row = iota((160, 256), 0)
    back = onehot(row + jnp.where(row >= 128, 32, 0) == iota((160, 256), 1))

    def turn(m):
        even, odd = acc[0, m], acc[1, m]
        total = jnp.concatenate(
            [even[:, :128] + odd[:, :128], even[:, 128:] + pltpu.roll(odd[:, 128:], 64, 1)], axis=1)
        high = total.astype(BF16)
        rest = (total - high.astype(F32)).astype(BF16)
        return [lax.dot_general(back, h, NT, preferred_element_type=F32) for h in (high, rest)]

    def copy5(m):
        return remote(part_out.at[m], part_in.at[m], s5.at[m], r5.at[m], sibling)

    def hand_over():
        for m in range(2):
            high, rest = turn(2 + m)
            part_out[m, 0] = high.astype(BF16)
            part_out[m, 1] = rest.astype(BF16)
            copy5(m).start()

    def chunk(n, places_of, edge):
        for s in range(STEPS):
            for i, (o, u) in enumerate(places_of):
                at = slice(16 * i, 16 * i + 16)
                pq[n % 2, s, at, :128] = buf[o, u, 2 * s]
                fq[n % 2, s, at, :128] = buf[o, u, 2 * s + 1]
                pq[n % 2, s, at, 128:] = buf[o, u, 4]
                fq[n % 2, s, at, 128:] = buf[o, u, 4]
        for ms in ((2, 3), (0, 1)):
            for s in range(STEPS):
                ends = edge(s)
                for m in ms:
                    mine = rows[s, m // 2, m % 2 * 5:m % 2 * 5 + 5].reshape(640, 256)
                    lf = left[m // 2, m % 2 * 5:m % 2 * 5 + 5].reshape(640, 128)
                    zeta = lax.dot_general(mine, pq[n % 2, s], NT, preferred_element_type=F32)
                    tri = jnp.concatenate(
                        [(zeta[:, 128 * i:128 * i + 128] / (lf + ends[i])).astype(BF16) for i in range(2)], axis=1)
                    term = jnp.dot(tri, fq[n % 2, s], preferred_element_type=F32)
                    if n == 0:
                        acc[s, m] = term
                    else:
                        acc[s, m] += term
            if n == 4 and ms[0] == 2:
                hand_over()

    def pair_of(o1, o2):
        return [(o, u) for o in (o1, o2) for u in range(8)], lambda s: [right[s, pl.ds(o, 1), :] for o in (o1, o2)]

    for part in range(5):
        for way in range(2):
            copy4(0, way, part, l).start()
    for t in range(1, 5):
        for part in range(5):
            for way in range(2):
                if t == 4 and way != part // 3:
                    continue
                origin = (l + t) & 7 if way else (l + 8 - t) & 7
                copy4(t - 1, way, part, origin).wait_recv()
                if t < 3 or (t == 3 and way == part // 3):
                    copy4(t, way, part, origin).start()
        if t < 4:
            chunk(t - 1, *pair_of((l + 8 - t) & 7, (l + t) & 7))
    chunk(3, *pair_of(l, (l + 4) & 7))
    chunk(4, [(o, u) for u in (8, 9) for o in range(8)], lambda s: [right[s, 8:9, :], right[s, 9:10, :]])

    for m in range(2):
        high, rest = turn(m)
        copy5(m).wait_recv()
        done = (high + part_in[m, 0].astype(F32) + (rest + part_in[m, 1].astype(F32))).astype(BF16)
        for a in range(5):
            out[5 * m + a] = done[:, 128 * a:128 * a + 120]

    @pl.loop(0, UNITS)
    def _(t):
        there, row_ = holder(t)

        @pl.when(row_ != yl)
        def _():
            copy1(t, row_).wait_send()

        @pl.when((row_ == yl) & (there != z))
        def _():
            copy2(t, there).wait_send()

        @pl.when((row_ == yl) & (there == z))
        def _():
            @pl.loop(1, 4)
            def _(i):
                copy3(slot_of(t), i).wait_send()

        @pl.when(source(t)[1] == f)
        def _():
            @pl.loop(1, 8)
            def _(i):
                copy6(t, i).wait_send()

    swap.wait_send()
    for t in range(4):
        for part in range(5):
            for way in range(2):
                if t == 3 and way != part // 3:
                    continue
                origin = (l + t) & 7 if way else (l + 8 - t) & 7
                copy4(t, way, part, origin).wait_send()
    for m in range(2):
        copy5(m).wait_send()


def local(amps, ints_pair, ints_fold, eps_occ, eps_vir, kconserve, plan):
    anywhere = pl.BlockSpec(memory_space=pl.ANY)
    dma = pltpu.SemaphoreType.DMA
    out = pl.pallas_call(
        kernel,
        out_shape=jax.ShapeDtypeStruct((10, 160, 120), BF16),
        in_specs=[anywhere] * 7,
        out_specs=pl.BlockSpec(memory_space=pltpu.VMEM),
        scratch_shapes=[
            pltpu.SMEM((2,), jnp.int32),
            pltpu.SMEM((64, 64), jnp.int32),
            pltpu.VMEM((2, 10, 160, 120), BF16),
            pltpu.VMEM((2, 10, 16, 160), BF16),
            pltpu.VMEM((2, 16, 32, 160), BF16),
            pltpu.VMEM((16, 64), F32),
            pltpu.VMEM((64, 160), F32),
            pltpu.VMEM((UNITS, 5, 16, 128), BF16),
            pltpu.VMEM((2, 2, 10, 128, 256), BF16),
            pltpu.VMEM((2, 10, 128, 128), F32),
            pltpu.VMEM((2, 16, 128), F32),
            pltpu.VMEM((4, UNITS, 5, 16, 128), BF16),
            pltpu.VMEM((8, UNITS, 5, 16, 128), BF16),
            pltpu.VMEM((2, 2, 256, 256), BF16),
            pltpu.VMEM((2, 2, 256, 256), BF16),
            pltpu.VMEM((2, 4, 640, 256), F32),
            pltpu.VMEM((2, 2, 160, 640), BF16),
            pltpu.VMEM((2, 2, 160, 640), BF16),
            pltpu.VMEM((UNITS, 5, 16, 128), BF16),
            pltpu.VMEM((8, UNITS, 5, 16, 128), BF16),
            dma((7,)),
            dma((UNITS,)), dma((4, UNITS)),
            dma((UNITS,)), dma((8, UNITS)),
            dma((1,)), dma((1,)),
            dma((4, 2, 5)), dma((4, 2, 5)),
            dma((2,)), dma((2,)),
            dma((4, UNITS)), dma((UNITS,)),
            dma((8, UNITS)), dma((UNITS,)),
        ],
        compiler_params=pltpu.CompilerParams(
            vmem_limit_bytes=56 * 2**20, collective_id=0, has_side_effects=True),
        name="triples",
    )(plan, kconserve, jnp.transpose(amps, (0, 2, 3, 1))[0], jnp.transpose(ints_pair, (0, 3, 2, 1)),
      ints_fold, eps_occ.T, eps_vir)
    return jnp.transpose(out, (2, 0, 1))[None]


def solution(mesh):
    return jax.shard_map(
        local,
        mesh=mesh,
        in_specs=(
            P("kb", None, "vir", None),
            P("kb", None, None, "vir"),
            P("kb", None, None, None),
            P(),
            P(),
            P(),
            P(),
        ),
        out_specs=P("kb", None, "vir", None),
        check_vma=False,
    )
```

```python
import functools

import jax
import jax.numpy as jnp
import numpy as np
from jax import lax
from jax.experimental import pallas as pl
from jax.experimental.pallas import tpu as pltpu
from jax.sharding import PartitionSpec as P

STEPS = 2
UNITS = 10
MESH = pl.DeviceIdType.MESH
F32 = jnp.float32
BF16 = jnp.bfloat16
NT = (((1,), (1,)), ((), ()))
TN = (((0,), (0,)), ((), ()))


def iota(shape, dim):
    return lax.broadcasted_iota(jnp.int32, shape, dim)


def onehot(mask):
    return jnp.where(mask, 1.0, 0.0).astype(BF16)


def kernel(plan_any, kcons_any, amps_any, pair_any, fold_any, occt_any, evir_any, out,
           plan, kcons, amps, pair, fold, occt, evir, x, rows, left, right, cand, buf, pq, fq, acc, part_out, part_in,
           mid, got, s0, s1, r1, s2, r2, s3, r3, s4, r4, s5, r5, s6, r6, s7, r7, s8, r8):
    kb = lax.axis_index("kb")
    vir = lax.axis_index("vir")
    z, yl = kb >> 2, kb & 3
    xx, yh, core = vir >> 2, (vir >> 1) & 1, vir & 1
    y = yh * 4 + yl
    flip = core == 1
    f = jnp.where(flip, z, y)
    l = jnp.where(flip, y, z)
    kfirst = 2 * kb

    def dev(x_, f_, l_):
        y_ = jnp.where(flip, l_, f_)
        z_ = jnp.where(flip, f_, l_)
        return (z_ * 4 + (y_ & 3), x_ * 4 + (y_ >> 2) * 2 + core)

    def holder(t):
        v8 = xx * 2 + yh
        last = t >= 8
        z0 = jnp.where(last, v8, t)
        y0 = (z0 + xx + jnp.where(last, t - 7, 0)) & 3
        z1 = jnp.where(last, (xx + 4 * t - 30) & 7, (t & 1) * 4 + xx)
        y1 = jnp.where(last, xx, t >> 1)
        return jnp.where(flip, z1, z0), jnp.where(flip, y1, y0)

    def source(u):
        last = u >= 8
        v8 = jnp.where(last, l, u)
        y0 = (v8 & 1) * 4 + ((l + (v8 >> 1) + jnp.where(last, u - 7, 0)) & 3)
        ll = l & 3
        x1 = jnp.where(last, ll, u & 3)
        z1 = jnp.where(last, (ll + 4 * u - 30) & 7, u)
        return jnp.where(flip, x1, v8 >> 1), jnp.where(flip, z1, y0)

    sibling = (kb, vir + 1 - 2 * core)
    rnext = dev(xx, f, (l + 1) & 7)
    lnext = dev(xx, f, (l + 7) & 7)
    across = dev(xx, f, (l + 4) & 7)

    low = pl.multiple_of(jnp.minimum((10 * vir >> 4) << 4, 128), 16)
    loads = [
        pltpu.make_async_copy(fold_any.at[:, :, pl.ds(low, 32)], fold, s0.at[0]),
        pltpu.make_async_copy(pair_any, pair, s0.at[1]),
        pltpu.make_async_copy(amps_any, amps.at[0], s0.at[2]),
        pltpu.make_async_copy(occt_any, occt, s0.at[3]),
        pltpu.make_async_copy(evir_any, evir, s0.at[4]),
        pltpu.make_async_copy(kcons_any, kcons, s0.at[5]),
        pltpu.make_async_copy(plan_any, plan, s0.at[6]),
    ]
    for c in loads:
        c.start()

    barrier = pltpu.get_barrier_semaphore()

    def far(i):
        step = (i + 1) >> 1
        return 4 - jnp.where((i & 1) == 1, step, -step)

    def greet(d):
        pl.semaphore_signal(barrier, inc=1, device_id=d, device_id_type=MESH)

    @pl.loop(0, 7)
    def _(i):
        greet((((z + far(i)) & 7) * 4 + yl, vir))
        greet(dev(xx, (f + far(i)) & 7, l))

    @pl.loop(1, 4)
    def _(i):
        greet((z * 4 + ((yl + i) & 3), vir))
        greet(dev((xx + i) & 3, f, l))

    greet(across)
    greet(rnext)
    greet(lnext)
    greet(sibling)

    pick = onehot(
        (iota((160, 512), 0) % 16 == iota((160, 512), 1) // 32)
        & (iota((160, 512), 1) % 32 + low == 10 * vir + iota((160, 512), 0) // 16)
    )
    row, col = iota((160, 128), 0), iota((160, 128), 1)
    tail = [onehot((row - 128 == col - 32 * j) & (row >= 128)) for j in range(4)]
    dot = functools.partial(jnp.dot, preferred_element_type=F32)
    loads[6].wait()
    loads[0].wait()
    loads[1].wait()
    rem = None
    for s in range(STEPS):
        at = plan[s] % 2
        p = pair[at]
        g = dot(pick, fold[at].reshape(512, 160)).astype(BF16)
        x[:, 2 * s] = p[:, :, :128]
        x[:, 2 * s + 1] = g[:, :128].reshape(10, 16, 128)
        ends = dot(p.reshape(160, 160), tail[2 * s]) + dot(g, tail[2 * s + 1])
        rem = ends if rem is None else rem + ends
    x[:, 4] = rem.astype(BF16).reshape(10, 16, 128)
    loads[2].wait()

    pl.semaphore_wait(barrier, 3 + 7 + 3 + 7 + 3 + 1)

    def remote(src, dst, ss, rs, d):
        return pltpu.make_async_remote_copy(
            src_ref=src, dst_ref=dst, send_sem=ss, recv_sem=rs, device_id=d, device_id_type=MESH)

    def copy1(t, there):
        return remote(x.at[t], cand.at[yl, t], s1.at[t], r1.at[yl, t], (z * 4 + there, vir))

    @pl.loop(0, UNITS)
    def _(t):
        there = holder(t)[1]

        @pl.when(there != yl)
        def _():
            copy1(t, there).start()

        @pl.when(there == yl)
        def _():
            cand[yl, t] = x[t]

    swap = remote(amps.at[0], amps.at[1], s3.at[0], r3.at[0], sibling)
    swap.start()

    loads[3].wait()
    loads[4].wait()
    loads[5].wait()
    row, band = iota((128, 16), 0), iota((128, 16), 1)
    member = jnp.zeros((128, 16), jnp.bool_)
    start = 0
    for i in range(16):
        inside = (row >= start) & (row < start + 15 - i)
        member = member | (inside & ((band == i) | (band == i + 1 + row - start)))
        start += 15 - i
    exact = dict(precision=lax.Precision.HIGHEST, preferred_element_type=F32)
    sums = jnp.dot(jnp.where(member, 1.0, 0.0), occt[...], **exact)
    pe = jnp.sum(jnp.where(iota((128, 64), 1) == kfirst, sums, 0.0), axis=1, keepdims=True)
    level = iota((64, 160), 0)
    vrow = jnp.sum(jnp.where(level == kfirst, evir[...], 0.0), axis=0, keepdims=True)
    for who in range(2):
        owner = vir + who * (1 - 2 * core)
        for a in range(10):
            mine = jnp.sum(jnp.where(iota((1, 160), 1) == 10 * owner + a, vrow, 0.0), axis=1, keepdims=True)
            left[who, a] = jnp.broadcast_to(mine - pe, (128, 128))
    lane = iota((160, 128), 1)
    w = lane // 16
    v16 = jnp.where(flip, (w % 4 * 2 + w // 4) * 2 + 1, 2 * w)
    spread = jnp.where(iota((160, 128), 0) // 10 == v16, 1.0, 0.0)
    occ16 = lax.dot_general(
        occt[...], jnp.where(iota((16, 128), 1) % 16 == iota((16, 128), 0), 1.0, 0.0), TN, **exact)
    half = iota((1, 128), 1) < 64
    for s in range(STEPS):
        k3 = plan[s]
        k2 = kcons[kfirst, k3]
        vs = jnp.sum(jnp.where(level == k2, evir[...], 0.0), axis=0, keepdims=True)
        own = jnp.where(iota((16, 160), 1) % 10 == iota((16, 160), 0), vs, 0.0)
        occ = jnp.sum(jnp.where(iota((64, 128), 0) == k3, occ16, 0.0), axis=0, keepdims=True)
        table = jnp.dot(own, spread, **exact) - occ
        turned = pltpu.roll(table, 64, 1)
        for o in range(8):
            t = 2 * (o % 4)
            if o < 4:
                both = jnp.where(half, table[t:t + 1], turned[t + 1:t + 2])
            else:
                both = jnp.where(half, turned[t:t + 1], table[t + 1:t + 2])
            right[s, o:o + 1, :] = jnp.where(flip, both, table[o:o + 1])
        right[s, 8:10, :] = table[8:10]

    e, to = iota((160, 256), 0), iota((160, 256), 1)
    places = [onehot(e + jnp.where(e >= 128, 64 * s, 0) == to) for s in range(STEPS)]

    def lay(who):
        for s in range(STEPS):
            for a in range(10):
                rows[s, who, a, :120] = lax.dot_general(
                    amps[who, a], places[s], TN, preferred_element_type=F32).astype(BF16)
                rows[s, who, a, 120:] = jnp.zeros((8, 256), BF16)

    first, second = plan[0] // 2, plan[1] // 2
    split = iota((16, 128), 1) < 64

    def copy2(t, there):
        return remote(mid.at[t], got.at[z, t], s2.at[t], r2.at[z, t], (there * 4 + yl, vir))

    @pl.loop(0, UNITS)
    def _(t):
        @pl.when(holder(t)[1] == yl)
        def _():
            @pl.loop(1, 4)
            def _(i):
                other = (yl + i) & 3
                remote(x.at[t], cand.at[other, t], s1.at[t], r1.at[other, t], (z * 4 + yl, vir)).wait_recv()

    @pl.loop(0, UNITS)
    def _(t):
        there, row_ = holder(t)

        @pl.when(row_ == yl)
        def _():
            one, two = first & 3, second & 3
            mid[t, 0] = cand[one, t, 0]
            mid[t, 1] = cand[one, t, 1]
            mid[t, 2] = cand[two, t, 2]
            mid[t, 3] = cand[two, t, 3]
            mid[t, 4] = jnp.where(split, cand[one, t, 4].astype(F32), cand[two, t, 4].astype(F32)).astype(BF16)

            @pl.when(there != z)
            def _():
                copy2(t, there).start()

            @pl.when(there == z)
            def _():
                got[z, t] = mid[t]

    lay(0)

    def slot_of(t):
        u0 = jnp.where(t >= 8, t, xx * 2 + yh)
        u1 = jnp.where(t >= 8, t, (t & 1) * 4 + xx)
        return jnp.where(flip, u1, u0)

    def copy3(u, i):
        here = buf.at[l, u]
        return remote(here, here, s6.at[i, u], r6.at[u], dev((xx + i) & 3, f, l))

    @pl.loop(0, UNITS)
    def _(t):
        there, row_ = holder(t)

        @pl.when((row_ == yl) & (there == z))
        def _():
            @pl.loop(1, 8)
            def _(i):
                other = (z + i) & 7
                remote(mid.at[t], got.at[other, t], s2.at[t], r2.at[other, t], (z * 4 + yl, vir)).wait_recv()

            one, two = first >> 2, second >> 2
            u = slot_of(t)
            buf[l, u, 0] = got[one, t, 0]
            buf[l, u, 1] = got[one, t, 1]
            buf[l, u, 2] = got[two, t, 2]
            buf[l, u, 3] = got[two, t, 3]
            buf[l, u, 4] = jnp.where(split, got[one, t, 4].astype(F32), got[two, t, 4].astype(F32)).astype(BF16)

            @pl.loop(1, 4)
            def _(i):
                copy3(u, 4 - i).start()

    def copy6(u, i):
        here = buf.at[l, u]
        return remote(here, here, s7.at[i, u], r7.at[u], dev(xx, (f + i) & 7, l))

    @pl.loop(0, UNITS)
    def _(u):
        a, b = source(u)

        @pl.when(b == f)
        def _():
            @pl.when(a != xx)
            def _():
                copy3(u, 1).wait_recv()

            @pl.loop(0, 7)
            def _(i):
                copy6(u, far(i)).start()

    swap.wait_recv()
    lay(1)

    def copy4(t, way, part, origin):
        here = buf.at[origin, pl.ds(2 * part, 2)]
        return remote(here, here, s4.at[t, way, part], r4.at[t, way, part], lnext if way else rnext)

    def copy8(origin):
        here = buf.at[origin]
        return remote(here, here, s8.at[0], r8.at[0], across)

    row = iota((160, 256), 0)
    back = onehot(row + jnp.where(row >= 128, 32, 0) == iota((160, 256), 1))

    def turn(m):
        even, odd = acc[0, m], acc[1, m]
        total = jnp.concatenate(
            [even[:, :128] + odd[:, :128], even[:, 128:] + pltpu.roll(odd[:, 128:], 64, 1)], axis=1)
        high = total.astype(BF16)
        rest = (total - high.astype(F32)).astype(BF16)
        return [lax.dot_general(back, h, NT, preferred_element_type=F32) for h in (high, rest)]

    def copy5(m):
        return remote(part_out.at[m], part_in.at[m], s5.at[m], r5.at[m], sibling)

    def hand_over():
        for m in range(2):
            high, rest = turn(2 + m)
            part_out[m, 0] = high.astype(BF16)
            part_out[m, 1] = rest.astype(BF16)
            copy5(m).start()

    def chunk(n, places_of, edge):
        for s in range(STEPS):
            for i, (o, u) in enumerate(places_of):
                at = slice(16 * i, 16 * i + 16)
                pq[n % 2, s, at, :128] = buf[o, u, 2 * s]
                fq[n % 2, s, at, :128] = buf[o, u, 2 * s + 1]
                pq[n % 2, s, at, 128:] = buf[o, u, 4]
                fq[n % 2, s, at, 128:] = buf[o, u, 4]
        for ms in ((2, 3), (0, 1)):
            for s in range(STEPS):
                ends = edge(s)
                for m in ms:
                    mine = rows[s, m // 2, m % 2 * 5:m % 2 * 5 + 5].reshape(640, 256)
                    lf = left[m // 2, m % 2 * 5:m % 2 * 5 + 5].reshape(640, 128)
                    zeta = lax.dot_general(mine, pq[n % 2, s], NT, preferred_element_type=F32)
                    tri = jnp.concatenate(
                        [(zeta[:, 128 * i:128 * i + 128] / (lf + ends[i])).astype(BF16) for i in range(2)], axis=1)
                    term = jnp.dot(tri, fq[n % 2, s], preferred_element_type=F32)
                    if n == 0:
                        acc[s, m] = term
                    else:
                        acc[s, m] += term
            if n == 4 and ms[0] == 2:
                hand_over()

    def pair_of(o1, o2):
        return [(o, u) for o in (o1, o2) for u in range(8)], lambda s: [right[s, pl.ds(o, 1), :] for o in (o1, o2)]

    for part in range(5):
        for u in (2 * part, 2 * part + 1):
            @pl.when(source(u)[1] != f)
            def _(u=u):
                copy6(u, 1).wait_recv()

        for way in range(2):
            copy4(0, way, part, l).start()
    copy8(l).start()
    for t in range(1, 4):
        if t == 3:
            copy8((l + 4) & 7).wait_recv()
            chunk(2, *pair_of(l, (l + 4) & 7))
        for part in range(5):
            for way in range(2):
                origin = (l + t) & 7 if way else (l + 8 - t) & 7
                copy4(t - 1, way, part, origin).wait_recv()
                if t < 3:
                    copy4(t, way, part, origin).start()
        chunk(t if t == 3 else t - 1, *pair_of((l + 8 - t) & 7, (l + t) & 7))
    chunk(4, [(o, u) for u in (8, 9) for o in range(8)], lambda s: [right[s, 8:9, :], right[s, 9:10, :]])

    for m in range(2):
        high, rest = turn(m)
        copy5(m).wait_recv()
        done = (high + part_in[m, 0].astype(F32) + (rest + part_in[m, 1].astype(F32))).astype(BF16)
        for a in range(5):
            out[5 * m + a] = done[:, 128 * a:128 * a + 120]

    @pl.loop(0, UNITS)
    def _(t):
        there, row_ = holder(t)

        @pl.when(row_ != yl)
        def _():
            copy1(t, row_).wait_send()

        @pl.when((row_ == yl) & (there != z))
        def _():
            copy2(t, there).wait_send()

        @pl.when((row_ == yl) & (there == z))
        def _():
            @pl.loop(1, 4)
            def _(i):
                copy3(slot_of(t), i).wait_send()

        @pl.when(source(t)[1] == f)
        def _():
            @pl.loop(1, 8)
            def _(i):
                copy6(t, i).wait_send()

    swap.wait_send()
    copy8(l).wait_send()
    for t in range(3):
        for part in range(5):
            for way in range(2):
                origin = (l + t) & 7 if way else (l + 8 - t) & 7
                copy4(t, way, part, origin).wait_send()
    for m in range(2):
        copy5(m).wait_send()


def local(amps, ints_pair, ints_fold, eps_occ, eps_vir, kconserve, plan):
    anywhere = pl.BlockSpec(memory_space=pl.ANY)
    dma = pltpu.SemaphoreType.DMA
    out = pl.pallas_call(
        kernel,
        out_shape=jax.ShapeDtypeStruct((10, 160, 120), BF16),
        in_specs=[anywhere] * 7,
        out_specs=pl.BlockSpec(memory_space=pltpu.VMEM),
        scratch_shapes=[
            pltpu.SMEM((2,), jnp.int32),
            pltpu.SMEM((64, 64), jnp.int32),
            pltpu.VMEM((2, 10, 160, 120), BF16),
            pltpu.VMEM((2, 10, 16, 160), BF16),
            pltpu.VMEM((2, 16, 32, 160), BF16),
            pltpu.VMEM((16, 64), F32),
            pltpu.VMEM((64, 160), F32),
            pltpu.VMEM((UNITS, 5, 16, 128), BF16),
            pltpu.VMEM((2, 2, 10, 128, 256), BF16),
            pltpu.VMEM((2, 10, 128, 128), F32),
            pltpu.VMEM((2, 16, 128), F32),
            pltpu.VMEM((4, UNITS, 5, 16, 128), BF16),
            pltpu.VMEM((8, UNITS, 5, 16, 128), BF16),
            pltpu.VMEM((2, 2, 256, 256), BF16),
            pltpu.VMEM((2, 2, 256, 256), BF16),
            pltpu.VMEM((2, 4, 640, 256), F32),
            pltpu.VMEM((2, 2, 160, 640), BF16),
            pltpu.VMEM((2, 2, 160, 640), BF16),
            pltpu.VMEM((UNITS, 5, 16, 128), BF16),
            pltpu.VMEM((8, UNITS, 5, 16, 128), BF16),
            dma((7,)),
            dma((UNITS,)), dma((4, UNITS)),
            dma((UNITS,)), dma((8, UNITS)),
            dma((1,)), dma((1,)),
            dma((3, 2, 5)), dma((3, 2, 5)),
            dma((2,)), dma((2,)),
            dma((4, UNITS)), dma((UNITS,)),
            dma((8, UNITS)), dma((UNITS,)),
            dma((1,)), dma((1,)),
        ],
        compiler_params=pltpu.CompilerParams(
            vmem_limit_bytes=56 * 2**20, collective_id=0, has_side_effects=True),
        name="triples",
    )(plan, kconserve, jnp.transpose(amps, (0, 2, 3, 1))[0], jnp.transpose(ints_pair, (0, 3, 2, 1)),
      ints_fold, eps_occ.T, eps_vir)
    return jnp.transpose(out, (2, 0, 1))[None]


def solution(mesh):
    return jax.shard_map(
        local,
        mesh=mesh,
        in_specs=(
            P("kb", None, "vir", None),
            P("kb", None, None, "vir"),
            P("kb", None, None, None),
            P(),
            P(),
            P(),
            P(),
        ),
        out_specs=P("kb", None, "vir", None),
        check_vma=False,
    )
```

```python
import functools

import jax
import jax.numpy as jnp
import numpy as np
from jax import lax
from jax.experimental import pallas as pl
from jax.experimental.pallas import tpu as pltpu
from jax.sharding import PartitionSpec as P

STEPS = 2
UNITS = 10
MESH = pl.DeviceIdType.MESH
F32 = jnp.float32
BF16 = jnp.bfloat16
NT = (((1,), (1,)), ((), ()))
TN = (((0,), (0,)), ((), ()))


def iota(shape, dim):
    return lax.broadcasted_iota(jnp.int32, shape, dim)


def onehot(mask):
    return jnp.where(mask, 1.0, 0.0).astype(BF16)


def kernel(plan_any, kcons_any, amps_any, pair_any, fold_any, occt_any, evir_any, out,
           plan, kcons, amps, pair, fold, occt, evir, x, rows, left, right, cand, buf, pq, fq, acc, part_out, part_in,
           mid, got, s0, s1, r1, s2, r2, s3, r3, s4, r4, s5, r5, s6, r6, s7, r7, s8, r8):
    kb = lax.axis_index("kb")
    vir = lax.axis_index("vir")
    z, yl = kb >> 2, kb & 3
    xx, yh, core = vir >> 2, (vir >> 1) & 1, vir & 1
    y = yh * 4 + yl
    flip = core == 1
    f = jnp.where(flip, z, y)
    l = jnp.where(flip, y, z)
    kfirst = 2 * kb

    def dev(x_, f_, l_):
        y_ = jnp.where(flip, l_, f_)
        z_ = jnp.where(flip, f_, l_)
        return (z_ * 4 + (y_ & 3), x_ * 4 + (y_ >> 2) * 2 + core)

    def holder(t):
        v8 = xx * 2 + yh
        last = t >= 8
        z0 = jnp.where(last, v8, t)
        y0 = (z0 + xx + jnp.where(last, t - 7, 0)) & 3
        z1 = jnp.where(last, (xx + 4 * t - 30) & 7, (t & 1) * 4 + xx)
        y1 = jnp.where(last, xx, t >> 1)
        return jnp.where(flip, z1, z0), jnp.where(flip, y1, y0)

    def source(u):
        last = u >= 8
        v8 = jnp.where(last, l, u)
        y0 = (v8 & 1) * 4 + ((l + (v8 >> 1) + jnp.where(last, u - 7, 0)) & 3)
        ll = l & 3
        x1 = jnp.where(last, ll, u & 3)
        z1 = jnp.where(last, (ll + 4 * u - 30) & 7, u)
        return jnp.where(flip, x1, v8 >> 1), jnp.where(flip, z1, y0)

    sibling = (kb, vir + 1 - 2 * core)
    rnext = dev(xx, f, (l + 1) & 7)
    lnext = dev(xx, f, (l + 7) & 7)
    across = dev(xx, f, (l + 4) & 7)

    low = pl.multiple_of(jnp.minimum((10 * vir >> 4) << 4, 128), 16)
    loads = [
        pltpu.make_async_copy(fold_any.at[:, :, pl.ds(low, 32)], fold, s0.at[0]),
        pltpu.make_async_copy(pair_any, pair, s0.at[1]),
        pltpu.make_async_copy(amps_any, amps.at[0], s0.at[2]),
        pltpu.make_async_copy(occt_any, occt, s0.at[3]),
        pltpu.make_async_copy(evir_any, evir, s0.at[4]),
        pltpu.make_async_copy(kcons_any, kcons, s0.at[5]),
        pltpu.make_async_copy(plan_any, plan, s0.at[6]),
    ]
    for c in loads:
        c.start()

    barrier = pltpu.get_barrier_semaphore()

    def far(i):
        step = (i + 1) >> 1
        return 4 - jnp.where((i & 1) == 1, step, -step)

    def greet(d):
        pl.semaphore_signal(barrier, inc=1, device_id=d, device_id_type=MESH)

    @pl.loop(0, 7)
    def _(i):
        greet((((z + far(i)) & 7) * 4 + yl, vir))
        greet(dev(xx, (f + far(i)) & 7, l))

    @pl.loop(1, 4)
    def _(i):
        greet((z * 4 + ((yl + i) & 3), vir))
        greet(dev((xx + i) & 3, f, l))

    greet(across)
    greet(rnext)
    greet(lnext)
    greet(sibling)

    pick = onehot(
        (iota((160, 512), 0) % 16 == iota((160, 512), 1) // 32)
        & (iota((160, 512), 1) % 32 + low == 10 * vir + iota((160, 512), 0) // 16)
    )
    row, col = iota((160, 128), 0), iota((160, 128), 1)
    tail = [onehot((row - 128 == col - 32 * j) & (row >= 128)) for j in range(4)]
    dot = functools.partial(jnp.dot, preferred_element_type=F32)
    loads[6].wait()
    loads[0].wait()
    loads[1].wait()
    rem = None
    for s in range(STEPS):
        at = plan[s] % 2
        p = pair[at]
        g = dot(pick, fold[at].reshape(512, 160)).astype(BF16)
        x[:, 2 * s] = p[:, :, :128]
        x[:, 2 * s + 1] = g[:, :128].reshape(10, 16, 128)
        ends = dot(p.reshape(160, 160), tail[2 * s]) + dot(g, tail[2 * s + 1])
        rem = ends if rem is None else rem + ends
    x[:, 4] = rem.astype(BF16).reshape(10, 16, 128)
    loads[2].wait()

    pl.semaphore_wait(barrier, 3 + 7 + 3 + 7 + 3 + 1)

    def remote(src, dst, ss, rs, d):
        return pltpu.make_async_remote_copy(
            src_ref=src, dst_ref=dst, send_sem=ss, recv_sem=rs, device_id=d, device_id_type=MESH)

    def copy1(t, there):
        return remote(x.at[t], cand.at[yl, t], s1.at[t], r1.at[yl, t], (z * 4 + there, vir))

    @pl.loop(0, UNITS)
    def _(t):
        there = holder(t)[1]

        @pl.when(there != yl)
        def _():
            copy1(t, there).start()

        @pl.when(there == yl)
        def _():
            cand[yl, t] = x[t]

    swap = remote(amps.at[0], amps.at[1], s3.at[0], r3.at[0], sibling)
    swap.start()

    loads[3].wait()
    loads[4].wait()
    loads[5].wait()
    row, band = iota((128, 16), 0), iota((128, 16), 1)
    member = jnp.zeros((128, 16), jnp.bool_)
    start = 0
    for i in range(16):
        inside = (row >= start) & (row < start + 15 - i)
        member = member | (inside & ((band == i) | (band == i + 1 + row - start)))
        start += 15 - i
    exact = dict(precision=lax.Precision.HIGHEST, preferred_element_type=F32)
    sums = jnp.dot(jnp.where(member, 1.0, 0.0), occt[...], **exact)
    pe = jnp.sum(jnp.where(iota((128, 64), 1) == kfirst, sums, 0.0), axis=1, keepdims=True)
    level = iota((64, 160), 0)
    vrow = jnp.sum(jnp.where(level == kfirst, evir[...], 0.0), axis=0, keepdims=True)
    for who in range(2):
        owner = vir + who * (1 - 2 * core)
        for a in range(10):
            mine = jnp.sum(jnp.where(iota((1, 160), 1) == 10 * owner + a, vrow, 0.0), axis=1, keepdims=True)
            left[who, a] = jnp.broadcast_to(mine - pe, (128, 128))
    lane = iota((160, 128), 1)
    w = lane // 16
    v16 = jnp.where(flip, (w % 4 * 2 + w // 4) * 2 + 1, 2 * w)
    spread = jnp.where(iota((160, 128), 0) // 10 == v16, 1.0, 0.0)
    occ16 = lax.dot_general(
        occt[...], jnp.where(iota((16, 128), 1) % 16 == iota((16, 128), 0), 1.0, 0.0), TN, **exact)
    half = iota((1, 128), 1) < 64
    for s in range(STEPS):
        k3 = plan[s]
        k2 = kcons[kfirst, k3]
        vs = jnp.sum(jnp.where(level == k2, evir[...], 0.0), axis=0, keepdims=True)
        own = jnp.where(iota((16, 160), 1) % 10 == iota((16, 160), 0), vs, 0.0)
        occ = jnp.sum(jnp.where(iota((64, 128), 0) == k3, occ16, 0.0), axis=0, keepdims=True)
        table = jnp.dot(own, spread, **exact) - occ
        turned = pltpu.roll(table, 64, 1)
        for o in range(8):
            t = 2 * (o % 4)
            if o < 4:
                both = jnp.where(half, table[t:t + 1], turned[t + 1:t + 2])
            else:
                both = jnp.where(half, turned[t:t + 1], table[t + 1:t + 2])
            right[s, o:o + 1, :] = jnp.where(flip, both, table[o:o + 1])
        right[s, 8:10, :] = table[8:10]

    e, to = iota((160, 256), 0), iota((160, 256), 1)
    places = [onehot(e + jnp.where(e >= 128, 64 * s, 0) == to) for s in range(STEPS)]

    def lay(who):
        for s in range(STEPS):
            for a in range(10):
                rows[s, who, a, :120] = lax.dot_general(
                    amps[who, a], places[s], TN, preferred_element_type=F32).astype(BF16)
                rows[s, who, a, 120:] = jnp.zeros((8, 256), BF16)

    first, second = plan[0] // 2, plan[1] // 2
    split = iota((16, 128), 1) < 64

    def copy2(t, there):
        return remote(mid.at[t], got.at[z, t], s2.at[t], r2.at[z, t], (there * 4 + yl, vir))

    @pl.loop(0, UNITS)
    def _(t):
        @pl.when(holder(t)[1] == yl)
        def _():
            @pl.loop(1, 4)
            def _(i):
                other = (yl + i) & 3
                remote(x.at[t], cand.at[other, t], s1.at[t], r1.at[other, t], (z * 4 + yl, vir)).wait_recv()

    @pl.loop(0, UNITS)
    def _(t):
        there, row_ = holder(t)

        @pl.when(row_ == yl)
        def _():
            one, two = first & 3, second & 3
            mid[t, 0] = cand[one, t, 0]
            mid[t, 1] = cand[one, t, 1]
            mid[t, 2] = cand[two, t, 2]
            mid[t, 3] = cand[two, t, 3]
            mid[t, 4] = jnp.where(split, cand[one, t, 4].astype(F32), cand[two, t, 4].astype(F32)).astype(BF16)

            @pl.when(there != z)
            def _():
                copy2(t, there).start()

            @pl.when(there == z)
            def _():
                got[z, t] = mid[t]

    lay(0)

    def slot_of(t):
        u0 = jnp.where(t >= 8, t, xx * 2 + yh)
        u1 = jnp.where(t >= 8, t, (t & 1) * 4 + xx)
        return jnp.where(flip, u1, u0)

    def copy3(u, i):
        here = buf.at[l, u]
        return remote(here, here, s6.at[i, u], r6.at[u], dev((xx + i) & 3, f, l))

    @pl.loop(0, UNITS)
    def _(t):
        there, row_ = holder(t)

        @pl.when((row_ == yl) & (there == z))
        def _():
            @pl.loop(1, 8)
            def _(i):
                other = (z + i) & 7
                remote(mid.at[t], got.at[other, t], s2.at[t], r2.at[other, t], (z * 4 + yl, vir)).wait_recv()

            one, two = first >> 2, second >> 2
            u = slot_of(t)
            buf[l, u, 0] = got[one, t, 0]
            buf[l, u, 1] = got[one, t, 1]
            buf[l, u, 2] = got[two, t, 2]
            buf[l, u, 3] = got[two, t, 3]
            buf[l, u, 4] = jnp.where(split, got[one, t, 4].astype(F32), got[two, t, 4].astype(F32)).astype(BF16)

            @pl.loop(1, 4)
            def _(i):
                copy3(u, 4 - i).start()

    def copy6(u, i):
        here = buf.at[l, u]
        return remote(here, here, s7.at[i, u], r7.at[u], dev(xx, (f + i) & 7, l))

    @pl.loop(0, UNITS)
    def _(u):
        a, b = source(u)

        @pl.when(b == f)
        def _():
            @pl.when(a != xx)
            def _():
                copy3(u, 1).wait_recv()

            @pl.loop(0, 7)
            def _(i):
                copy6(u, far(i)).start()

    swap.wait_recv()
    lay(1)

    def copy4(t, way, part, origin):
        here = buf.at[origin, pl.ds(2 * part, 2)]
        return remote(here, here, s4.at[t, way, part], r4.at[t, way, part], lnext if way else rnext)

    def copy8(origin):
        here = buf.at[origin]
        return remote(here, here, s8.at[0], r8.at[0], across)

    row = iota((160, 256), 0)
    back = onehot(row + jnp.where(row >= 128, 32, 0) == iota((160, 256), 1))

    def turn(m):
        even, odd = acc[0, m], acc[1, m]
        total = jnp.concatenate(
            [even[:, :128] + odd[:, :128], even[:, 128:] + pltpu.roll(odd[:, 128:], 64, 1)], axis=1)
        high = total.astype(BF16)
        rest = (total - high.astype(F32)).astype(BF16)
        return [lax.dot_general(back, h, NT, preferred_element_type=F32) for h in (high, rest)]

    def copy5(m):
        return remote(part_out.at[m], part_in.at[m], s5.at[m], r5.at[m], sibling)

    def hand_over():
        for m in range(2):
            high, rest = turn(2 + m)
            part_out[m, 0] = high.astype(BF16)
            part_out[m, 1] = rest.astype(BF16)
            copy5(m).start()

    def chunk(n, places_of, edge):
        for s in range(STEPS):
            for i, (o, u) in enumerate(places_of):
                at = slice(16 * i, 16 * i + 16)
                pq[n % 2, s, at, :128] = buf[o, u, 2 * s]
                fq[n % 2, s, at, :128] = buf[o, u, 2 * s + 1]
                pq[n % 2, s, at, 128:] = buf[o, u, 4]
                fq[n % 2, s, at, 128:] = buf[o, u, 4]
        for ms in ((2, 3), (0, 1)):
            for s in range(STEPS):
                ends = edge(s)
                for m in ms:
                    mine = rows[s, m // 2, m % 2 * 5:m % 2 * 5 + 5].reshape(640, 256)
                    lf = left[m // 2, m % 2 * 5:m % 2 * 5 + 5].reshape(640, 128)
                    zeta = lax.dot_general(mine, pq[n % 2, s], NT, preferred_element_type=F32)
                    tri = jnp.concatenate(
                        [(zeta[:, 128 * i:128 * i + 128] / (lf + ends[i])).astype(BF16) for i in range(2)], axis=1)
                    term = jnp.dot(tri, fq[n % 2, s], preferred_element_type=F32)
                    if n == 0:
                        acc[s, m] = term
                    else:
                        acc[s, m] += term
            if n == 4 and ms[0] == 2:
                hand_over()

    def pair_of(o1, o2):
        return [(o, u) for o in (o1, o2) for u in range(8)], lambda s: [right[s, pl.ds(o, 1), :] for o in (o1, o2)]

    for part in range(5):
        for u in (2 * part, 2 * part + 1):
            @pl.when(source(u)[1] != f)
            def _(u=u):
                copy6(u, 1).wait_recv()

        for way in range(2):
            copy4(0, way, part, l).start()
    copy8(l).start()
    for t in range(1, 4):
        if t == 3:
            copy8((l + 4) & 7).wait_recv()
            chunk(2, *pair_of(l, (l + 4) & 7))
        for part in range(5):
            for way in range(2):
                origin = (l + t) & 7 if way else (l + 8 - t) & 7
                copy4(t - 1, way, part, origin).wait_recv()
                if t < 3:
                    copy4(t, way, part, origin).start()
        chunk(t if t == 3 else t - 1, *pair_of((l + 8 - t) & 7, (l + t) & 7))
    chunk(4, [(o, u) for u in (8, 9) for o in range(8)], lambda s: [right[s, 8:9, :], right[s, 9:10, :]])

    for m in range(2):
        high, rest = turn(m)
        copy5(m).wait_recv()
        done = (high + part_in[m, 0].astype(F32) + (rest + part_in[m, 1].astype(F32))).astype(BF16)
        for a in range(5):
            out[5 * m + a] = done[:, 128 * a:128 * a + 120]

    @pl.loop(0, UNITS)
    def _(t):
        there, row_ = holder(t)

        @pl.when(row_ != yl)
        def _():
            copy1(t, row_).wait_send()

        @pl.when((row_ == yl) & (there != z))
        def _():
            copy2(t, there).wait_send()

        @pl.when((row_ == yl) & (there == z))
        def _():
            @pl.loop(1, 4)
            def _(i):
                copy3(slot_of(t), i).wait_send()

        @pl.when(source(t)[1] == f)
        def _():
            @pl.loop(1, 8)
            def _(i):
                copy6(t, i).wait_send()

    swap.wait_send()
    copy8(l).wait_send()
    for t in range(3):
        for part in range(5):
            for way in range(2):
                origin = (l + t) & 7 if way else (l + 8 - t) & 7
                copy4(t, way, part, origin).wait_send()
    for m in range(2):
        copy5(m).wait_send()


def local(amps, ints_pair, ints_fold, eps_occ, eps_vir, kconserve, plan):
    anywhere = pl.BlockSpec(memory_space=pl.ANY)
    dma = pltpu.SemaphoreType.DMA
    out = pl.pallas_call(
        kernel,
        out_shape=pltpu.VMEM((10, 160, 120), BF16),
        in_specs=[anywhere] * 7,
        out_specs=pl.BlockSpec(memory_space=pltpu.VMEM),
        scratch_shapes=[
            pltpu.SMEM((2,), jnp.int32),
            pltpu.SMEM((64, 64), jnp.int32),
            pltpu.VMEM((2, 10, 160, 120), BF16),
            pltpu.VMEM((2, 10, 16, 160), BF16),
            pltpu.VMEM((2, 16, 32, 160), BF16),
            pltpu.VMEM((16, 64), F32),
            pltpu.VMEM((64, 160), F32),
            pltpu.VMEM((UNITS, 5, 16, 128), BF16),
            pltpu.VMEM((2, 2, 10, 128, 256), BF16),
            pltpu.VMEM((2, 10, 128, 128), F32),
            pltpu.VMEM((2, 16, 128), F32),
            pltpu.VMEM((4, UNITS, 5, 16, 128), BF16),
            pltpu.VMEM((8, UNITS, 5, 16, 128), BF16),
            pltpu.VMEM((2, 2, 256, 256), BF16),
            pltpu.VMEM((2, 2, 256, 256), BF16),
            pltpu.VMEM((2, 4, 640, 256), F32),
            pltpu.VMEM((2, 2, 160, 640), BF16),
            pltpu.VMEM((2, 2, 160, 640), BF16),
            pltpu.VMEM((UNITS, 5, 16, 128), BF16),
            pltpu.VMEM((8, UNITS, 5, 16, 128), BF16),
            dma((7,)),
            dma((UNITS,)), dma((4, UNITS)),
            dma((UNITS,)), dma((8, UNITS)),
            dma((1,)), dma((1,)),
            dma((3, 2, 5)), dma((3, 2, 5)),
            dma((2,)), dma((2,)),
            dma((4, UNITS)), dma((UNITS,)),
            dma((8, UNITS)), dma((UNITS,)),
            dma((1,)), dma((1,)),
        ],
        compiler_params=pltpu.CompilerParams(
            vmem_limit_bytes=56 * 2**20, collective_id=0, has_side_effects=True),
        name="triples",
    )(plan, kconserve, jnp.transpose(amps, (0, 2, 3, 1))[0], jnp.transpose(ints_pair, (0, 3, 2, 1)),
      ints_fold, eps_occ.T, eps_vir)
    return jnp.transpose(out, (2, 0, 1))[None]


def solution(mesh):
    return jax.shard_map(
        local,
        mesh=mesh,
        in_specs=(
            P("kb", None, "vir", None),
            P("kb", None, None, "vir"),
            P("kb", None, None, None),
            P(),
            P(),
            P(),
            P(),
        ),
        out_specs=P("kb", None, "vir", None),
        check_vma=False,
    )
```
